256 devices in a mesh: rows: 32 (over z_hi, y, core), rep: 8 (over x, z_lo).
Axes of the slice: x: 4, y: 4, z: 8 (z_hi: 4, z_lo: 2; z = z_hi * 2 + z_lo), core: 2. Of those that a mesh axis runs over, the one named last changes fastest.
Arguments:
- features: bfloat16 [32768, 256], P('rows'), as said below
- weight: bfloat16 [256, 256], replicated, may hold values from -0.375 to 0.375
- cotangent: bfloat16 [32768, 256], P('rows'), may hold values from -6 to 6
- node_order: int32 [32, 1024], P('rows'), may hold values from 0 to 1023, each once within a row
- forward_tiles: bfloat16 [32, 8, 4, 32, 128, 128], P('rows', 'rep'), as said below
- forward_slots: int32 [32, 8, 4, 2, 32], P('rows', 'rep'), may hold values from 0 to 7, as said below
- forward_count: int32 [32, 8, 4], P('rows', 'rep'), may hold values from 1 to 32, as said below
- backward_tiles: bfloat16 [32, 8, 4, 32, 128, 128], P('rows', 'rep'), as said below
- backward_slots: int32 [32, 8, 4, 2, 32], P('rows', 'rep'), may hold values from 0 to 7, as said below
- backward_count: int32 [32, 8, 4], P('rows', 'rep'), may hold values from 1 to 32, as said below
Outputs:
- layer_output: bfloat16 [32768, 256], P('rows')
- grad_weight: float32 [256, 256], replicated
- grad_input: bfloat16 [32768, 256], P('rows')
The draws below stay inside these ranges and needn't reach their ends.
Inputs may be any that keep to these rules, and one draw needn't show every extreme that they name: `node_order`: each row names every position of its row block once. forward_slots[i, r, t, 0, s] and forward_slots[i, r, t, 1, s] are the row tile and the column tile of slot s of the pair of row block i and column block t * 8 + r; the 32 slots of one pair name distinct tiles. `forward_count`: at most 32 live slots a pair, exactly 32 for some pair. `forward_tiles`: slots at or beyond a pair's count hold values that are not part of the operator. backward_tiles[j, r, t, s] is forward_tiles[i, j % 8, j // 8, s] transposed, with i = t * 8 + r. backward_slots[j, r, t, 0, s] = forward_slots[i, j % 8, j // 8, 1, s] and backward_slots[j, r, t, 1, s] = forward_slots[i, j % 8, j // 8, 0, s], with i = t * 8 + r. backward_count[j, r, t] = forward_count[i, j % 8, j // 8], with i = t * 8 + r. `features`: nonnegative.
All inputs are finite; a program needn't handle non-finite values.
Results may differ from the reference program's by a relative error of at most 0.0051.
Values may be sent and summed in bfloat16 or wider, within the bound.
A program may use at most 128 MiB of HBM per device.

```python
import math
import jax
import jax.numpy as jnp
from jax import lax

FEAT = 256
HID = 256
TILE = 128
BLOCK = 1024
CAP = 32
SECTIONS = 4
NODES = 32768
N_ROWS = 32
N_REP = 8


def pair_count(key, row_block, col_block):
    level_key = jax.random.fold_in(jax.random.fold_in(key, 21), row_block)
    load_level = jax.random.randint(level_key, (), 2, 6)
    pair_key = jax.random.fold_in(jax.random.fold_in(key, 22), row_block * N_ROWS + col_block)
    base_draw = jax.random.randint(pair_key, (), 0, CAP + 1)
    drawn_count = jnp.minimum(CAP, 1 + base_draw * load_level // 4)
    hot_pair = jax.random.randint(jax.random.fold_in(key, 23), (), 0, N_ROWS * N_ROWS)
    return jnp.where(row_block * N_ROWS + col_block == hot_pair, CAP, drawn_count).astype(jnp.int32)


def pair_slots(key, row_block, col_block):
    tile_rows = BLOCK // TILE
    pair_key = jax.random.fold_in(jax.random.fold_in(key, 24), row_block * N_ROWS + col_block)
    shuffled = jax.random.permutation(pair_key, tile_rows * tile_rows)[:CAP].astype(jnp.int32)
    return (shuffled // tile_rows, shuffled % tile_rows)


def pair_tiles(key, row_block, col_block):
    tile_rows = BLOCK // TILE
    pair_key = jax.random.fold_in(jax.random.fold_in(key, 25), row_block * N_ROWS + col_block)
    values = jax.random.normal(pair_key, (CAP, TILE, TILE), jnp.float32)
    return values / jnp.sqrt(56.0 * SECTIONS * CAP / tile_rows)


def forward_layout(maker):
    rep_grid = jnp.arange(N_REP).astype(jnp.int32)[:, None]
    step_grid = jnp.arange(SECTIONS).astype(jnp.int32)[None, :]
    column_grid = step_grid * N_REP + rep_grid

    def per_row(row_block):
        return jax.vmap(jax.vmap(lambda col_block: maker(row_block, col_block)))(column_grid)
    return lax.map(per_row, jnp.arange(N_ROWS).astype(jnp.int32))


def backward_layout(maker):
    rep_grid = jnp.arange(N_REP).astype(jnp.int32)[:, None]
    step_grid = jnp.arange(SECTIONS).astype(jnp.int32)[None, :]
    source_grid = step_grid * N_REP + rep_grid

    def per_column(col_block):
        return jax.vmap(jax.vmap(lambda row_block: maker(row_block, col_block)))(source_grid)
    return lax.map(per_column, jnp.arange(N_ROWS).astype(jnp.int32))


def draw_features(key, part):
    key = jax.random.fold_in(key, 5)
    raw_values = jax.random.normal(key, (NODES, FEAT), jnp.float32) * 1.2 + 0.2
    return jnp.maximum(raw_values, 0.0).astype(jnp.bfloat16)


def draw_forward_tiles(key, part):
    return forward_layout(lambda row_block, col_block: pair_tiles(key, row_block, col_block).astype(jnp.bfloat16))


def draw_backward_tiles(key, part):
    return backward_layout(lambda row_block, col_block: jnp.swapaxes(pair_tiles(key, row_block, col_block), 1, 2).astype(jnp.bfloat16))


def draw_forward_slots(key, part):

    def maker(row_block, col_block):
        row_tiles, column_tiles = pair_slots(key, row_block, col_block)
        return jnp.stack([row_tiles, column_tiles])
    return forward_layout(maker)


def draw_backward_slots(key, part):

    def maker(row_block, col_block):
        row_tiles, column_tiles = pair_slots(key, row_block, col_block)
        return jnp.stack([column_tiles, row_tiles])
    return backward_layout(maker)


def draw_forward_count(key, part):
    return forward_layout(lambda row_block, col_block: pair_count(key, row_block, col_block))


def draw_backward_count(key, part):
    return backward_layout(lambda row_block, col_block: pair_count(key, row_block, col_block))


def block_scale(stream_key, dims, split, least, top_value):
    loudness = 1.0
    for position, shards_of in split:
        heights = jax.random.uniform(jax.random.fold_in(jax.random.fold_in(stream_key, 6), position), (shards_of,), jnp.float32, least / len(split), top_value / len(split))
        loudness = loudness * jnp.repeat(jnp.exp(heights), dims[position] // shards_of).reshape((-1,) + (1,) * (len(dims) - 1 - position))
    return loudness


def normal_values(rng, extent, deviation, reach, pieces=(), dtype=jnp.bfloat16):
    entries = jax.random.normal(rng, extent, jnp.float32) * deviation
    if len(pieces) > 0:
        entries = block_scale(rng, extent, pieces, -0.22, 0.18) * entries
    return jnp.clip(entries, min=-reach, max=reach).astype(dtype)


def setup_inputs(seed: int = 0) -> dict:
    streams_of = jax.random.split(jax.random.key(seed), 11)
    features = draw_features(jax.random.fold_in(streams_of[10], 71), 0)
    weight = normal_values(streams_of[1], (FEAT, HID), FEAT ** -0.5, 0.375)
    cotangent = normal_values(streams_of[2], (NODES, HID), 1.0, 6.0, ((0, 32),))
    node_order = jax.vmap(lambda own: jax.random.permutation(own, BLOCK))(jax.random.split(streams_of[3], N_ROWS)).reshape((N_ROWS, BLOCK)).astype(jnp.int32)
    forward_tiles = draw_forward_tiles(jax.random.fold_in(streams_of[10], 71), 0)
    forward_slots = draw_forward_slots(jax.random.fold_in(streams_of[10], 71), 0)
    forward_count = draw_forward_count(jax.random.fold_in(streams_of[10], 71), 0)
    backward_tiles = draw_backward_tiles(jax.random.fold_in(streams_of[10], 71), 0)
    backward_slots = draw_backward_slots(jax.random.fold_in(streams_of[10], 71), 0)
    backward_count = draw_backward_count(jax.random.fold_in(streams_of[10], 71), 0)
    return dict(features=features, weight=weight, cotangent=cotangent, node_order=node_order, forward_tiles=forward_tiles, forward_slots=forward_slots, forward_count=forward_count, backward_tiles=backward_tiles, backward_slots=backward_slots, backward_count=backward_count)


def section_product(source_block, tile_set, row_slots, column_slots, live_count):
    tile_size = tile_set.shape[-1]
    tile_rows = source_block.shape[0] // tile_size
    feature_count = source_block.shape[1]
    column_rows = source_block.reshape(tile_rows, tile_size, feature_count)[column_slots]
    products = jnp.einsum('cuv,cvf->cuf', tile_set.astype(jnp.float32), column_rows.astype(jnp.float32), precision=lax.Precision.HIGHEST)
    slot_index = jnp.arange(tile_set.shape[0]).astype(jnp.int32)
    row_index = jnp.arange(tile_rows).astype(jnp.int32)
    placement = ((row_slots[None, :] == row_index[:, None]) & (slot_index < live_count)[None, :]).astype(jnp.float32)
    summed = jnp.einsum('ac,cuf->auf', placement, products, precision=lax.Precision.HIGHEST)
    return summed.reshape(tile_rows * tile_size, feature_count)

def aggregate(source, tile_sets, slot_lists, live_counts):
    stacked = source.reshape(SECTIONS, N_REP, BLOCK, FEAT).transpose(1, 0, 2, 3)
    paired = jax.vmap(jax.vmap(section_product))

    def row_block(operands):
        tiles_here, slots_here, counts_here = operands
        terms = paired(stacked, tiles_here, slots_here[:, :, 0], slots_here[:, :, 1], counts_here)
        return lax.optimization_barrier(jnp.sum(terms, axis=(0, 1)))
    return lax.map(row_block, (tile_sets, slot_lists, live_counts)).reshape(NODES, FEAT)

def reference(features, weight, cotangent, node_order, forward_tiles, forward_slots, forward_count, backward_tiles, backward_slots, backward_count):
    blocked = features.reshape(N_ROWS, BLOCK, FEAT)
    reordered = jnp.take_along_axis(blocked, node_order[:, :, None], axis=1).reshape(NODES, FEAT)
    aggregated = aggregate(reordered, forward_tiles, forward_slots, forward_count).astype(jnp.bfloat16)
    layer_output = jnp.dot(aggregated, weight, preferred_element_type=jnp.float32).astype(jnp.bfloat16)
    grad_weight = jnp.dot(aggregated.T, cotangent, preferred_element_type=jnp.float32) * (1.0 / math.sqrt(NODES))
    back_rows = jnp.dot(cotangent, weight.T, preferred_element_type=jnp.float32).astype(jnp.bfloat16)
    grad_reordered = aggregate(back_rows, backward_tiles, backward_slots, backward_count).astype(jnp.bfloat16)

    def restore(values, index_row):
        return jnp.zeros_like(values).at[index_row].set(values)
    unpermuted = jax.vmap(restore)(grad_reordered.reshape(N_ROWS, BLOCK, FEAT), node_order).reshape(NODES, FEAT)
    grad_input = unpermuted * (features > 0).astype(jnp.bfloat16)
    return (layer_output, grad_weight, grad_input)
```

```python
import math

import jax
import jax.numpy as jnp
from jax import lax
from jax.experimental import pallas as pl
from jax.experimental.pallas import tpu as pltpu
from jax.sharding import PartitionSpec as P

F32 = jnp.float32
BF16 = jnp.bfloat16
MESH = pl.DeviceIdType.MESH

N_X = 4
N_Y = 4
N_T = 4
N_REP = 8
BLOCK = 1024
FEAT = 256
TILE = 128
GRID = BLOCK // TILE
CAP = 32
CHUNK = 256
CHUNKS = BLOCK // CHUNK
SHARE = BLOCK // N_REP
GROWS = FEAT // N_REP


def rows_index(t, y, core):
    return (t * N_Y + y) * 2 + core


def layer_kernel(
    scale,
    map_ref,
    order_hbm,
    feat_hbm,
    weight_hbm,
    cot_hbm,
    ftiles_hbm,
    btiles_hbm,
    lo_ref,
    gw_ref,
    gi_ref,
    order_v,
    feat_v,
    weight_v,
    cot_v,
    ftiles_v,
    btiles_v,
    dense,
    unperm,
    src,
    part,
    part_b,
    rs_land,
    share_v,
    gterm,
    ga_land,
    gb_land,
    gc_land,
    gd_land,
    gfin,
    local_sem,
    chunk_recv,
    y_send,
    z_send,
    f_send,
    s_send,
    rs_send,
    rs_recv,
    ag_send,
    ag_recv,
    ga_send,
    ga_recv,
    gb_send,
    gb_recv,
    gc_send,
    gc_recv,
    gd_send,
    gd_recv,
    ge_send,
    ge_recv,
    out_sem,
):
    me = lax.axis_index("rows")
    rep = lax.axis_index("rep")
    core = me % 2
    y = (me // 2) % N_Y
    t = me // (2 * N_Y)
    x = rep // 2
    zl = rep % 2
    other = 1 - core
    t_up = (t + 1) % N_T
    t_dn = (t + N_T - 1) % N_T
    t_far = (t + 2) % N_T
    on_row = y == x
    source = jnp.logical_and(on_row, core == zl)
    not_source = jnp.logical_not(source)

    sibling = (rows_index(t, y, other), rep)
    up = (rows_index(t_up, y, core), rep)
    down = (rows_index(t_dn, y, core), rep)

    def y_peer(d, c):
        return (rows_index(t, (y + d) % N_Y, c), rep)

    def z_peer(d):
        return (rows_index((t + d) % N_T, y, core), rep)

    def rep_index(d):
        dx, dz = d // 2, d % 2
        px = (x + dx) % N_X
        pz = (zl + dz) % 2
        return px * 2 + pz

    def rep_from(d):
        dx, dz = d // 2, d % 2
        return ((x + N_X - dx) % N_X) * 2 + (zl + dz) % 2

    def rep_peer(d):
        return (me, rep_index(d))

    def remote(source_ref, target_ref, send, recv, device):
        return pltpu.make_async_remote_copy(
            src_ref=source_ref,
            dst_ref=target_ref,
            send_sem=send,
            recv_sem=recv,
            device_id=device,
            device_id_type=MESH,
        )

    loads = [
        pltpu.make_async_copy(order_hbm, order_v, local_sem.at[0]),
        pltpu.make_async_copy(feat_hbm, feat_v, local_sem.at[1]),
        pltpu.make_async_copy(weight_hbm, weight_v, local_sem.at[2]),
        pltpu.make_async_copy(cot_hbm, cot_v, local_sem.at[3]),
        pltpu.make_async_copy(ftiles_hbm, ftiles_v.at[:, pl.ds(0, CAP)], local_sem.at[4]),
        pltpu.make_async_copy(btiles_hbm, btiles_v.at[:, pl.ds(0, CAP)], local_sem.at[5]),
    ]
    tiles = (ftiles_v, btiles_v)
    for held in tiles:
        for s in range(N_T):
            held[s, CAP] = jnp.zeros((TILE, TILE), BF16)
    for load in loads:
        load.start()

    barrier = pltpu.get_barrier_semaphore()
    partners = [sibling]
    partners += [y_peer(d, core) for d in range(1, N_Y)]
    partners += [y_peer(d, other) for d in range(1, N_Y)]
    partners += [z_peer(d) for d in range(1, N_T)]
    partners += [rep_peer(d) for d in range(1, N_REP)]
    for partner in partners:
        pl.semaphore_signal(barrier, inc=1, device_id=partner, device_id_type=MESH)
    loads[0].wait()
    pl.semaphore_wait(barrier, len(partners))

    def chunk(p, block, q):
        return src.at[p, block, pl.ds(q * CHUNK, CHUNK), :]

    def chunk_to(p, block, q, send, device):
        ref = chunk(p, block, q)
        return remote(ref, ref, send, chunk_recv.at[p, block, q], device)

    def chunk_wait(p, block, q):
        chunk_to(p, block, q, s_send.at[0, 0, 0], sibling).wait_recv()

    def source_copies(p, q):
        c = q // (CHUNKS // 2)
        copies = [chunk_to(p, t, q, y_send.at[p, q, d], y_peer(d, c)) for d in range(1, N_Y)]
        copies.append(chunk_to(p, t, q, y_send.at[p, q, 0], sibling))
        return copies

    def own_copies(p, j):
        q = core * 2 + j
        return [
            chunk_to(p, t, q, z_send.at[p, j, 0], up),
            chunk_to(p, t, q, z_send.at[p, j, 1], down),
        ]

    def side_copy(p, block, j):
        return chunk_to(p, block, core * 2 + j, s_send.at[p, block, j], sibling)

    def forward_copy(p, j):
        if j == 0:
            return chunk_to(p, t_dn, core * 2, f_send.at[p, 0], up)
        return chunk_to(p, t_up, core * 2 + 1, f_send.at[p, 1], down)

    def spread_own(p):
        for j in range(2):

            @pl.when(not_source)
            def _():
                chunk_wait(p, t, core * 2 + j)

            for copy in own_copies(p, j):
                copy.start()

            @pl.when(jnp.logical_not(on_row))
            def _():
                side_copy(p, t, j).start()

    def spread_neighbours(p):
        for j in range(2):
            chunk_wait(p, t_dn, core * 2 + j)
            if j == 0:
                forward_copy(p, 0).start()
            side_copy(p, t_dn, j).start()
            chunk_wait(p, t_up, core * 2 + j)
            if j == 1:
                forward_copy(p, 1).start()
            side_copy(p, t_up, j).start()

    def spread_far(p):
        for j in range(2):
            chunk_wait(p, t_far, core * 2 + j)
            side_copy(p, t_far, j).start()

    def wait_side(p, block):
        for j in range(2):
            chunk_wait(p, block, other * 2 + j)

    def product(p, block, first=False):
        half = BLOCK // 2

        @pl.loop(0, 2)
        def _(m):
            rows = pl.ds(pl.multiple_of(m * half, half), half)
            term = jnp.dot(dense[p, block, rows, :], src[p, block], preferred_element_type=F32)
            if first:
                part[rows, :] = term
            else:
                part[rows, :] += term

    def lay_out(p):
        loads[4 + p].wait()

        @pl.loop(0, N_T * GRID)
        def _(step):
            s = step // GRID
            a = step % GRID
            rows = pl.ds(pl.multiple_of(a * TILE, TILE), TILE)
            for b in range(GRID):
                slot = map_ref[p, s, a * GRID + b]
                dense[p, s, rows, pl.ds(b * TILE, TILE)] = tiles[p][s, slot]

    @pl.when(source)
    def _():
        loads[1].wait()
        order_cols = jnp.transpose(jnp.broadcast_to(order_v[...], (TILE, BLOCK)))
        lanes = lax.broadcasted_iota(jnp.int32, (CHUNK, TILE), 1)
        for q in range(CHUNKS):
            wanted = order_cols[q * CHUNK : (q + 1) * CHUNK, :]
            one_hot = jnp.concatenate(
                [jnp.where(wanted == lanes + b * TILE, 1.0, 0.0).astype(BF16) for b in range(GRID)],
                axis=1,
            )
            picked = jnp.dot(one_hot, feat_v[...], preferred_element_type=F32)
            src[0, t, pl.ds(q * CHUNK, CHUNK), :] = picked.astype(BF16)
            for copy in source_copies(0, q):
                copy.start()

    @pl.when(not_source)
    def _():
        loads[1].wait()

    spread_own(0)
    loads[2].wait()
    loads[3].wait()

    @pl.when(source)
    def _():
        for q in range(CHUNKS):
            rows = pl.ds(q * CHUNK, CHUNK)
            back = lax.dot_general(
                cot_v[rows, :], weight_v[...], (((1,), (1,)), ((), ())), preferred_element_type=F32
            )
            src[1, t, rows, :] = back.astype(BF16)
            for copy in source_copies(1, q):
                copy.start()

    lay_out(0)

    def wait_rest(p):
        @pl.when(jnp.logical_not(source))
        def _():
            wait_side(p, t)

    wait_rest(0)
    product(0, t, first=True)
    spread_neighbours(0)
    spread_own(1)
    wait_side(0, t_dn)
    product(0, t_dn)
    wait_side(0, t_up)
    product(0, t_up)
    spread_far(0)
    wait_side(0, t_far)
    product(0, t_far)

    def share_rows(index):
        return pl.ds(pl.multiple_of(index * SHARE, SHARE), SHARE)

    def rs_copy(p, d):
        return remote(
            part_b.at[p, share_rows(rep_index(d)), :],
            rs_land.at[p, d],
            rs_send.at[p, d],
            rs_recv.at[p, d],
            rep_peer(d),
        )

    def ag_copy(p, out, d):
        return remote(
            share_v.at[p],
            out.at[share_rows(rep), :],
            ag_send.at[p, d],
            ag_recv.at[p, d],
            rep_peer(d),
        )

    def ag_wait(p, out, d):
        remote(
            share_v.at[p],
            out.at[share_rows(rep_from(d)), :],
            ag_send.at[p, d],
            ag_recv.at[p, d],
            rep_peer(d),
        ).wait_recv()

    part_b[0] = part[...].astype(BF16)
    for d in range(1, N_REP):
        rs_copy(0, d).start()

    lay_out(1)
    wait_rest(1)

    @pl.loop(0, GRID)
    def _(a):
        rows = pl.ds(pl.multiple_of(a * TILE, TILE), TILE)
        spots = lax.broadcasted_iota(jnp.int32, (TILE, BLOCK), 0) + a * TILE
        unperm[rows, :] = jnp.where(order_v[...] == spots, 1.0, 0.0).astype(BF16)

    def share_sum(p, own):
        total = own
        for d in range(1, N_REP):
            rs_copy(p, d).wait_recv()
            total = total + rs_land[p, d].astype(F32)
        return total

    total = share_sum(0, part[share_rows(rep), :])
    agg = total.astype(BF16)
    share_v[0] = jnp.dot(agg, weight_v[...], preferred_element_type=F32).astype(BF16)
    for d in range(1, N_REP):
        ag_copy(0, lo_ref, d).start()
    lo_own = pltpu.make_async_copy(share_v.at[0], lo_ref.at[share_rows(rep), :], out_sem.at[0])
    lo_own.start()

    gterm[...] = lax.dot_general(
        agg, cot_v[share_rows(rep), :], (((0,), (0,)), ((), ())), preferred_element_type=F32
    )

    def g_rows(index):
        return pl.ds(pl.multiple_of(index * GROWS, GROWS), GROWS)

    def ga_copy(d):
        return remote(
            gterm.at[g_rows(rep_index(d)), :],
            ga_land.at[d],
            ga_send.at[d],
            ga_recv.at[d],
            rep_peer(d),
        )

    for d in range(1, N_REP):
        ga_copy(d).start()

    product(1, t, first=True)
    spread_neighbours(1)
    wait_side(1, t_dn)
    product(1, t_dn)

    gsum = gterm[g_rows(rep), :]
    for d in range(1, N_REP):
        ga_copy(d).wait_recv()
        gsum = gsum + ga_land[d]

    def gb_copy(d):
        return remote(gb_land.at[y], gb_land.at[y], gb_send.at[d], gb_recv.at[d], y_peer(d, core))

    def gc_copy(d):
        return remote(gc_land.at[t], gc_land.at[t], gc_send.at[d], gc_recv.at[d], z_peer(d))

    def gd_copy():
        return remote(gd_land.at[core], gd_land.at[core], gd_send.at[0], gd_recv.at[0], sibling)

    def ge_copy(d):
        return remote(
            gfin, gw_ref.at[g_rows(rep), :], ge_send.at[d], ge_recv.at[d], rep_peer(d)
        )

    gb_land[y] = gsum
    for d in range(1, N_Y):
        gb_copy(d).start()

    wait_side(1, t_up)
    product(1, t_up)
    spread_far(1)

    for d in range(1, N_Y):
        gb_copy(d).wait_recv()
    gc_land[t] = gb_land[0] + gb_land[1] + gb_land[2] + gb_land[3]
    for d in range(1, N_T):
        gc_copy(d).start()

    wait_side(1, t_far)
    product(1, t_far)

    part_b[1] = part[...].astype(BF16)

    half = BLOCK // 2

    @pl.loop(0, 2)
    def _(m):
        rows = pl.ds(pl.multiple_of(m * half, half), half)
        part[rows, :] = jnp.dot(unperm[rows, :], part_b[1], preferred_element_type=F32)

    part_b[1] = part[...].astype(BF16)
    for d in range(1, N_REP):
        rs_copy(1, d).start()

    for d in range(1, N_T):
        gc_copy(d).wait_recv()
    gd_land[core] = gc_land[0] + gc_land[1] + gc_land[2] + gc_land[3]
    gd_copy().start()

    back_total = share_sum(1, part[share_rows(rep), :])
    keep = feat_v[share_rows(rep), :].astype(F32) > 0.0
    share_v[1] = jnp.where(keep, back_total, 0.0).astype(BF16)
    for d in range(1, N_REP):
        ag_copy(1, gi_ref, d).start()
    gi_own = pltpu.make_async_copy(share_v.at[1], gi_ref.at[share_rows(rep), :], out_sem.at[1])
    gi_own.start()

    gd_copy().wait_recv()
    gfin[...] = (gd_land[0] + gd_land[1]) * scale
    for d in range(1, N_REP):
        ge_copy(d).start()
    gw_own = pltpu.make_async_copy(gfin, gw_ref.at[g_rows(rep), :], out_sem.at[2])
    gw_own.start()

    for d in range(1, N_REP):
        ag_wait(0, lo_ref, d)
        ag_wait(1, gi_ref, d)
        ge_copy(d).wait_recv()
    lo_own.wait()
    gi_own.wait()
    gw_own.wait()

    for p in range(2):

        @pl.when(source)
        def _():
            for q in range(CHUNKS):
                for copy in source_copies(p, q):
                    copy.wait_send()

        for j in range(2):
            for copy in own_copies(p, j):
                copy.wait_send()
            forward_copy(p, j).wait_send()

            @pl.when(jnp.logical_not(on_row))
            def _():
                side_copy(p, t, j).wait_send()

            for block in (t_dn, t_up, t_far):
                side_copy(p, block, j).wait_send()
        for d in range(1, N_REP):
            rs_copy(p, d).wait_send()
            ag_copy(p, lo_ref, d).wait_send()
    for d in range(1, N_REP):
        ga_copy(d).wait_send()
        ge_copy(d).wait_send()
    for d in range(1, N_Y):
        gb_copy(d).wait_send()
    for d in range(1, N_T):
        gc_copy(d).wait_send()
    gd_copy().wait_send()


def slot_map(slots, count):
    index = jnp.arange(CAP, dtype=jnp.int32)
    key = slots[:, 0] * GRID + slots[:, 1]
    key = jnp.where(index[None, :] < count[:, None], key, -1)
    hit = key[:, :, None] == jnp.arange(GRID * GRID, dtype=jnp.int32)
    return jnp.min(jnp.where(hit, index[None, :, None], CAP), axis=1)


def body(
    features,
    weight,
    cotangent,
    node_order,
    forward_tiles,
    forward_slots,
    forward_count,
    backward_tiles,
    backward_slots,
    backward_count,
):
    maps = jnp.stack(
        [
            slot_map(forward_slots[0, 0], forward_count[0, 0]),
            slot_map(backward_slots[0, 0], backward_count[0, 0]),
        ]
    )
    scale = 1.0 / math.sqrt(BLOCK * lax.axis_size("rows"))
    any_spec = pl.BlockSpec(memory_space=pl.ANY)
    dma = pltpu.SemaphoreType.DMA

    def kernel(*refs):
        layer_kernel(scale, *refs)

    return pl.pallas_call(
        kernel,
        out_shape=[
            jax.ShapeDtypeStruct((BLOCK, FEAT), BF16),
            jax.ShapeDtypeStruct((FEAT, FEAT), F32),
            jax.ShapeDtypeStruct((BLOCK, FEAT), BF16),
        ],
        in_specs=[pl.BlockSpec(memory_space=pltpu.SMEM)] + [any_spec] * 6,
        out_specs=[any_spec] * 3,
        scratch_shapes=[
            pltpu.VMEM((1, BLOCK), jnp.int32),
            pltpu.VMEM((BLOCK, FEAT), BF16),
            pltpu.VMEM((FEAT, FEAT), BF16),
            pltpu.VMEM((BLOCK, FEAT), BF16),
            pltpu.VMEM((N_T, CAP + 1, TILE, TILE), BF16),
            pltpu.VMEM((N_T, CAP + 1, TILE, TILE), BF16),
            pltpu.VMEM((2, N_T, BLOCK, BLOCK), BF16),
            pltpu.VMEM((BLOCK, BLOCK), BF16),
            pltpu.VMEM((2, N_T, BLOCK, FEAT), BF16),
            pltpu.VMEM((BLOCK, FEAT), F32),
            pltpu.VMEM((2, BLOCK, FEAT), BF16),
            pltpu.VMEM((2, N_REP, SHARE, FEAT), BF16),
            pltpu.VMEM((2, SHARE, FEAT), BF16),
            pltpu.VMEM((FEAT, FEAT), F32),
            pltpu.VMEM((N_REP, GROWS, FEAT), F32),
            pltpu.VMEM((N_Y, GROWS, FEAT), F32),
            pltpu.VMEM((N_T, GROWS, FEAT), F32),
            pltpu.VMEM((2, GROWS, FEAT), F32),
            pltpu.VMEM((GROWS, FEAT), F32),
            dma((6,)),
            dma((2, N_T, CHUNKS)),
            dma((2, CHUNKS, N_Y)),
            dma((2, 2, 2)),
            dma((2, 2)),
            dma((2, N_T, 2)),
            dma((2, N_REP)),
            dma((2, N_REP)),
            dma((2, N_REP)),
            dma((2, N_REP)),
            dma((N_REP,)),
            dma((N_REP,)),
            dma((N_Y,)),
            dma((N_Y,)),
            dma((N_T,)),
            dma((N_T,)),
            dma((1,)),
            dma((1,)),
            dma((N_REP,)),
            dma((N_REP,)),
            dma((3,)),
        ],
        compiler_params=pltpu.CompilerParams(
            collective_id=0, has_side_effects=True, vmem_limit_bytes=56 * 1024 * 1024
        ),
    )(
        maps,
        node_order,
        features,
        weight,
        cotangent,
        forward_tiles[0, 0],
        backward_tiles[0, 0],
    )


def solution(mesh):
    placed = (
        P("rows", None),
        P(),
        P("rows", None),
        P("rows", None),
        P("rows", "rep", None, None, None, None),
        P("rows", "rep", None, None, None),
        P("rows", "rep", None),
        P("rows", "rep", None, None, None, None),
        P("rows", "rep", None, None, None),
        P("rows", "rep", None),
    )
    return jax.shard_map(
        body,
        mesh=mesh,
        in_specs=placed,
        out_specs=(P("rows", None), P(), P("rows", None)),
        check_vma=False,
    )
```

```python
import math

import jax
import jax.numpy as jnp
from jax import lax
from jax.experimental import pallas as pl
from jax.experimental.pallas import tpu as pltpu
from jax.sharding import PartitionSpec as P

F32 = jnp.float32
BF16 = jnp.bfloat16
MESH = pl.DeviceIdType.MESH

N_X = 4
N_Y = 4
N_T = 4
N_REP = 8
BLOCK = 1024
FEAT = 256
TILE = 128
GRID = BLOCK // TILE
CAP = 32
SHARE = BLOCK // N_REP
PART_A = 48
PART_B = SHARE - PART_A
GROWS = FEAT // 2 // N_REP


def rows_index(t, y, core):
    return (t * N_Y + y) * 2 + core


def layer_kernel(
    scale,
    fcount_ref,
    bcount_ref,
    fslots_hbm,
    bslots_hbm,
    order_hbm,
    feat_hbm,
    weight_hbm,
    cot_hbm,
    ftiles_hbm,
    btiles_hbm,
    lo_ref,
    gw_ref,
    gi_ref,
    slots_v,
    map_v,
    map_ref,
    order_v,
    feat_v,
    weight_v,
    cot_v,
    ftiles_v,
    btiles_v,
    dense,
    unperm,
    src,
    own,
    land_ya,
    land_xa,
    land_yb,
    part,
    part_b,
    rsx_land,
    rsz_land,
    rs_mid,
    rsz_out,
    rs_land,
    share_v,
    gterm,
    gd_land,
    gmid,
    ga_land,
    gb_land,
    gc_land,
    ghalf,
    local_sem,
    ya_send,
    ya_recv,
    xa_send,
    xa_recv,
    za_send,
    za_recv,
    zb_send,
    zb_recv,
    yb_send,
    yb_recv,
    xb_send,
    xb_recv,
    side_send,
    side_recv,
    rsx_send,
    rsx_recv,
    rsz_send,
    rsz_recv,
    agz_send,
    rs_send,
    rs_recv,
    ag_send,
    ag_recv,
    ga_send,
    ga_recv,
    gb_send,
    gb_recv,
    gc_send,
    gc_recv,
    gd_send,
    gd_recv,
    ge_send,
    ge_recv,
    gf_send,
    gf_recv,
    out_sem,
):
    me = lax.axis_index("rows")
    rep = lax.axis_index("rep")
    core = me % 2
    y = (me // 2) % N_Y
    t = me // (2 * N_Y)
    x = rep // 2
    zl = rep % 2
    other = 1 - core
    straight = core == zl
    crossed = jnp.logical_not(straight)
    blocks = [(t + d) % N_T for d in (0, 1, 3, 2)]

    sibling = (rows_index(t, y, other), rep)

    def y_peer(d):
        return (rows_index(t, (y + d) % N_Y, core), rep)

    def cross_peer(d):
        return (rows_index((t + d) % N_T, y, zl), x * 2 + core)

    def z_peer(d):
        return (rows_index((t + d) % N_T, y, core), rep)

    def rep_index(d):
        dx, dz = d // 2, d % 2
        px = (x + dx) % N_X
        pz = (zl + dz) % 2
        return px * 2 + pz

    def rep_from(d):
        dx, dz = d // 2, d % 2
        return ((x + N_X - dx) % N_X) * 2 + (zl + dz) % 2

    def rep_peer(d):
        return (me, rep_index(d))

    def remote(source_ref, target_ref, send, recv, device):
        return pltpu.make_async_remote_copy(
            src_ref=source_ref,
            dst_ref=target_ref,
            send_sem=send,
            recv_sem=recv,
            device_id=device,
            device_id_type=MESH,
        )

    loads = [
        pltpu.make_async_copy(order_hbm, order_v, local_sem.at[0]),
        pltpu.make_async_copy(feat_hbm, feat_v, local_sem.at[1]),
        pltpu.make_async_copy(weight_hbm, weight_v, local_sem.at[2]),
        pltpu.make_async_copy(cot_hbm, cot_v, local_sem.at[3]),
        pltpu.make_async_copy(ftiles_hbm, ftiles_v.at[:, pl.ds(0, CAP)], local_sem.at[4]),
        pltpu.make_async_copy(btiles_hbm, btiles_v.at[:, pl.ds(0, CAP)], local_sem.at[5]),
        pltpu.make_async_copy(fslots_hbm, slots_v.at[0], local_sem.at[6]),
        pltpu.make_async_copy(bslots_hbm, slots_v.at[1], local_sem.at[7]),
    ]
    tiles = (ftiles_v, btiles_v)
    for held in tiles:
        for s in range(N_T):
            held[s, CAP] = jnp.zeros((TILE, TILE), BF16)
    for load in loads:
        load.start()

    barrier = pltpu.get_barrier_semaphore()
    partners = [sibling]
    partners += [y_peer(d) for d in range(1, N_Y)]
    partners += [z_peer(d) for d in range(1, N_T)]
    partners += [cross_peer(d) for d in range(1, N_T)]
    partners += [rep_peer(d) for d in range(1, N_REP)]
    for partner in partners:
        pl.semaphore_signal(barrier, inc=1, device_id=partner, device_id_type=MESH)

    @pl.when(crossed)
    def _():
        pl.semaphore_signal(barrier, inc=1, device_id=cross_peer(0), device_id_type=MESH)

    def share_rows(index):
        return pl.ds(pl.multiple_of(index * SHARE, SHARE), SHARE)

    loads[0].wait()
    wanted = jnp.transpose(jnp.broadcast_to(order_v[0:1, share_rows(rep)], (SHARE, SHARE)))
    lanes = lax.broadcasted_iota(jnp.int32, (SHARE, TILE), 1)
    one_hot = jnp.concatenate(
        [jnp.where(wanted == lanes + b * TILE, 1.0, 0.0).astype(BF16) for b in range(GRID)], axis=1
    )
    loads[1].wait()
    own[0] = jnp.dot(one_hot, feat_v[...], preferred_element_type=F32).astype(BF16)
    land_ya[0, y] = own[0, 0:PART_A, :]

    @pl.when(straight)
    def _():
        land_yb[0, y, t] = own[0, PART_A:SHARE, :]
        pl.semaphore_wait(barrier, len(partners))

    @pl.when(crossed)
    def _():
        pl.semaphore_wait(barrier, len(partners) + 1)

    first_a = pl.ds(0, PART_A)
    last_b = pl.ds(PART_A, PART_B)

    def ya_copy(p, d):
        ref = land_ya.at[p, y]
        return remote(ref, ref, ya_send.at[p, d], ya_recv.at[p, d], y_peer(d))

    def xa_copy(p, d):
        return remote(
            land_ya.at[p, (x + d) % N_X], land_xa.at[p, x], xa_send.at[p, d], xa_recv.at[p, d], rep_peer(2 * d)
        )

    def za_copy(p, d):
        return remote(
            land_xa.at[p],
            src.at[p, t, :, zl, first_a, :],
            za_send.at[p, d],
            za_recv.at[p, d],
            cross_peer(d),
        )

    def zb_copy(p, d):
        return remote(
            own.at[p, last_b, :], land_yb.at[p, y, t], zb_send.at[p, d], zb_recv.at[p, d], cross_peer(d)
        )

    def yb_copy(p, i, d):
        ref = land_yb.at[p, y, blocks[i]]
        return remote(ref, ref, yb_send.at[p, i, d], yb_recv.at[p, i, d], y_peer(d))

    def xb_copy(p, i, d):
        return remote(
            land_yb.at[p, (x + d) % N_X, blocks[i]],
            src.at[p, blocks[i], x, core, last_b, :],
            xb_send.at[p, i, d],
            xb_recv.at[p, i, d],
            rep_peer(2 * d),
        )

    def side_copy(p, i):
        ref = src.at[p, blocks[i], :, core]
        return remote(ref, ref, side_send.at[p, i], side_recv.at[p, i], sibling)

    from_z = (0, 3, 1, 2)

    def begin(p):
        for d in (2, 1, 3):
            zb_copy(p, d).start()

        @pl.when(crossed)
        def _():
            zb_copy(p, 0).start()

        for d in (2, 1, 3):
            ya_copy(p, d).start()

    def z_wait(copy, i):
        if i == 0:

            @pl.when(crossed)
            def _():
                copy.wait_recv()

        else:
            copy.wait_recv()

    def a_over_x(p):
        for d in (1, 2, 3):
            ya_copy(p, d).wait_recv()
        for d in (2, 1, 3):
            xa_copy(p, d).start()
        land_xa[p, x] = land_ya[p, x]

    def a_over_z(p):
        for d in (1, 2, 3):
            xa_copy(p, d).wait_recv()
        for d in (2, 1, 3):
            za_copy(p, d).start()

        @pl.when(crossed)
        def _():
            za_copy(p, 0).start()

        @pl.when(straight)
        def _():
            src[p, t, :, zl, first_a, :] = land_xa[p]

    def b_over_y(p):
        for i in range(N_T):
            z_wait(zb_copy(p, from_z[i]), i)
            for d in (2, 1, 3):
                yb_copy(p, i, d).start()

    def b_over_x(p):
        for i in range(N_T):
            for d in (1, 2, 3):
                yb_copy(p, i, d).wait_recv()
            for d in (2, 1, 3):
                xb_copy(p, i, d).start()
            src[p, blocks[i], x, core, last_b, :] = land_yb[p, x, blocks[i]]

    def finish(p, i):
        for d in (1, 2, 3):
            xb_copy(p, i, d).wait_recv()
        z_wait(za_copy(p, from_z[i]), i)
        side_copy(p, i).start()

    def use(p, i):
        side_copy(p, i).wait_recv()
        product(p, blocks[i], first=i == 0)

    def product(p, block, first=False):
        half = BLOCK // 2

        @pl.loop(0, 2)
        def _(m):
            rows = pl.ds(pl.multiple_of(m * half, half), half)
            term = jnp.dot(
                dense[p, block, rows, :], src[p, block].reshape(BLOCK, FEAT), preferred_element_type=F32
            )
            if first:
                part[rows, :] = term
            else:
                part[rows, :] += term

    def slot_maps():
        loads[6].wait()
        loads[7].wait()
        count_refs = (fcount_ref, bcount_ref)
        rows8 = lax.broadcasted_iota(jnp.int32, (2 * N_T, 1), 0)
        live = jnp.zeros((2 * N_T, 1), jnp.int32)
        for row in range(2 * N_T):
            live = jnp.where(rows8 == row, count_refs[row // N_T][row % N_T], live)
        keys = jnp.concatenate(
            [slots_v[p, s, 0:1, :] * GRID + slots_v[p, s, 1:2, :] for p in range(2) for s in range(N_T)],
            axis=0,
        )
        cells = lax.broadcasted_iota(jnp.int32, (2 * N_T, TILE), 1)
        found = jnp.full((2 * N_T, TILE), CAP, jnp.int32)
        for slot in range(CAP):
            hit = jnp.logical_and(keys[:, slot : slot + 1] == cells, live > slot)
            found = jnp.where(hit, slot, found)
        map_v[...] = found
        to_scalar = pltpu.make_async_copy(map_v, map_ref, local_sem.at[8])
        to_scalar.start()
        to_scalar.wait()

    def lay_out(p):
        loads[4 + p].wait()

        @pl.loop(0, N_T * GRID)
        def _(step):
            s = step // GRID
            a = step % GRID
            rows = pl.ds(pl.multiple_of(a * TILE, TILE), TILE)
            for b in range(GRID):
                slot = map_ref[p * N_T + s, a * GRID + b]
                dense[p, s, rows, pl.ds(b * TILE, TILE)] = tiles[p][s, slot]

    begin(0)
    loads[2].wait()
    loads[3].wait()
    own[1] = lax.dot_general(
        cot_v[share_rows(rep), :], weight_v[...], (((1,), (1,)), ((), ())), preferred_element_type=F32
    ).astype(BF16)
    land_ya[1, y] = own[1, 0:PART_A, :]

    @pl.when(straight)
    def _():
        land_yb[1, y, t] = own[1, PART_A:SHARE, :]

    slot_maps()
    a_over_x(0)
    b_over_y(0)
    a_over_z(0)
    lay_out(0)
    b_over_x(0)
    begin(1)
    finish(0, 0)
    finish(0, 1)
    use(0, 0)
    a_over_x(1)
    finish(0, 2)
    use(0, 1)
    finish(0, 3)
    b_over_y(1)
    use(0, 2)
    a_over_z(1)
    use(0, 3)

    def pair_rows(index):
        return pl.ds(pl.multiple_of(index * 2 * SHARE, 2 * SHARE), 2 * SHARE)

    def rsx_copy(d):
        return remote(
            part_b.at[0, pair_rows((x + d) % N_X), :],
            rsx_land.at[d],
            rsx_send.at[d],
            rsx_recv.at[d],
            rep_peer(2 * d),
        )

    def rsz_copy():
        return remote(rsz_out, rsz_land, rsz_send.at[0], rsz_recv.at[0], rep_peer(1))

    part_b[0] = part[...].astype(BF16)
    for d in (2, 1, 3):
        rsx_copy(d).start()

    lay_out(1)

    @pl.loop(0, GRID)
    def _(a):
        rows = pl.ds(pl.multiple_of(a * TILE, TILE), TILE)
        spots = lax.broadcasted_iota(jnp.int32, (TILE, BLOCK), 0) + a * TILE
        unperm[rows, :] = jnp.where(order_v[...] == spots, 1.0, 0.0).astype(BF16)

    total = part[pair_rows(x), :]
    for d in range(1, N_X):
        rsx_copy(d).wait_recv()
        total = total + rsx_land[d].astype(F32)
    rs_mid[...] = total
    rsz_out[...] = rs_mid[share_rows(1 - zl), :].astype(BF16)
    rsz_copy().start()

    b_over_x(1)
    finish(1, 0)

    partner = rep_index(1)

    def ag_own(d):
        return remote(
            share_v.at[0], lo_ref.at[share_rows(rep), :], ag_send.at[0, d], ag_recv.at[0, d], rep_peer(d)
        )

    def ag_pass(d):
        rows = share_rows(partner)
        return remote(
            lo_ref.at[rows, :], lo_ref.at[rows, :], agz_send.at[d], ag_recv.at[0, 2 * d + 1], rep_peer(2 * d)
        )

    rsz_copy().wait_recv()
    agg = (rs_mid[share_rows(zl), :] + rsz_land[...].astype(F32)).astype(BF16)
    share_v[0] = jnp.dot(agg, weight_v[...], preferred_element_type=F32).astype(BF16)
    for d in (1, 4, 2, 6):
        ag_own(d).start()
    lo_own = pltpu.make_async_copy(share_v.at[0], lo_ref.at[share_rows(rep), :], out_sem.at[0])
    lo_own.start()

    gterm[...] = lax.dot_general(
        agg, cot_v[share_rows(rep), :], (((0,), (0,)), ((), ())), preferred_element_type=F32
    )
    ghalf_rows = FEAT // 2

    def core_rows(index):
        return pl.ds(pl.multiple_of(index * ghalf_rows, ghalf_rows), ghalf_rows)

    def gd_copy():
        return remote(
            gterm.at[core_rows(other), :], gd_land, gd_send.at[0], gd_recv.at[0], sibling
        )

    def g_rows(index):
        return pl.ds(pl.multiple_of(index * GROWS, GROWS), GROWS)

    def ga_copy(d):
        return remote(
            gmid.at[g_rows(rep_index(d)), :],
            ga_land.at[d],
            ga_send.at[d],
            ga_recv.at[d],
            rep_peer(d),
        )

    def gb_copy(d):
        return remote(gb_land.at[y], gb_land.at[y], gb_send.at[d], gb_recv.at[d], y_peer(d))

    def gc_copy(d):
        return remote(gc_land.at[t], gc_land.at[t], gc_send.at[d], gc_recv.at[d], z_peer(d))

    def ge_copy(d):
        mine = ghalf.at[g_rows(rep), :]
        return remote(mine, mine, ge_send.at[d], ge_recv.at[d], rep_peer(d))

    def gf_copy():
        return remote(
            ghalf, gw_ref.at[core_rows(core), :], gf_send.at[0], gf_recv.at[0], sibling
        )

    gd_copy().start()

    use(1, 0)
    finish(1, 1)

    ag_own(1).wait_recv()
    for d in range(1, N_X):
        ag_pass(d).start()
    gd_copy().wait_recv()
    gmid[...] = gterm[core_rows(core), :] + gd_land[...]
    for d in range(1, N_REP):
        ga_copy(d).start()

    use(1, 1)
    finish(1, 2)
    finish(1, 3)

    gsum = gmid[g_rows(rep), :]
    for d in range(1, N_REP):
        ga_copy(d).wait_recv()
        gsum = gsum + ga_land[d]
    gb_land[y] = gsum
    for d in range(1, N_Y):
        gb_copy(d).start()

    use(1, 2)
    use(1, 3)
    part_b[1] = part[...].astype(BF16)
    half = BLOCK // 2

    @pl.loop(0, 2)
    def _(m):
        rows = pl.ds(pl.multiple_of(m * half, half), half)
        part[rows, :] = jnp.dot(unperm[rows, :], part_b[1], preferred_element_type=F32)

    part_b[1] = part[...].astype(BF16)

    def rs_copy(d):
        return remote(
            part_b.at[1, share_rows(rep_index(d)), :],
            rs_land.at[d],
            rs_send.at[d],
            rs_recv.at[d],
            rep_peer(d),
        )

    def ag_copy(d):
        return remote(
            share_v.at[1], gi_ref.at[share_rows(rep), :], ag_send.at[1, d], ag_recv.at[1, d], rep_peer(d)
        )

    far_first = (5, 4, 3, 7, 2, 6, 1)
    for d in far_first:
        rs_copy(d).start()

    for d in range(1, N_Y):
        gb_copy(d).wait_recv()
    gc_land[t] = gb_land[0] + gb_land[1] + gb_land[2] + gb_land[3]
    for d in range(1, N_T):
        gc_copy(d).start()

    back_total = part[share_rows(rep), :]
    for d in range(1, N_REP):
        rs_copy(d).wait_recv()
        back_total = back_total + rs_land[d].astype(F32)
    keep = feat_v[share_rows(rep), :].astype(F32) > 0.0
    share_v[1] = jnp.where(keep, back_total, 0.0).astype(BF16)
    for d in far_first:
        ag_copy(d).start()
    gi_own = pltpu.make_async_copy(share_v.at[1], gi_ref.at[share_rows(rep), :], out_sem.at[1])
    gi_own.start()

    for d in range(1, N_T):
        gc_copy(d).wait_recv()
    ghalf[g_rows(rep), :] = (gc_land[0] + gc_land[1] + gc_land[2] + gc_land[3]) * scale
    for d in range(1, N_REP):
        ge_copy(d).start()
    for d in range(1, N_REP):
        ge_copy(d).wait_recv()
    gf_copy().start()
    gw_own = pltpu.make_async_copy(ghalf, gw_ref.at[core_rows(core), :], out_sem.at[2])
    gw_own.start()

    for d in (2, 4, 6, 3, 5, 7):
        ag_own(d).wait_recv()
    for d in range(1, N_REP):
        ag_copy(d).wait_recv()
    gf_copy().wait_recv()
    lo_own.wait()
    gi_own.wait()
    gw_own.wait()

    for p in range(2):

        @pl.when(crossed)
        def _():
            zb_copy(p, 0).wait_send()
            za_copy(p, 0).wait_send()

        for d in (1, 2, 3):
            ya_copy(p, d).wait_send()
            xa_copy(p, d).wait_send()
            za_copy(p, d).wait_send()
            zb_copy(p, d).wait_send()
            for i in range(N_T):
                yb_copy(p, i, d).wait_send()
                xb_copy(p, i, d).wait_send()
        for i in range(N_T):
            side_copy(p, i).wait_send()
    for d in (1, 2, 4, 6):
        ag_own(d).wait_send()
    for d in range(1, N_X):
        rsx_copy(d).wait_send()
        ag_pass(d).wait_send()
    rsz_copy().wait_send()
    for d in range(1, N_REP):
        rs_copy(d).wait_send()
        ag_copy(d).wait_send()
        ga_copy(d).wait_send()
        ge_copy(d).wait_send()
    for d in range(1, N_Y):
        gb_copy(d).wait_send()
    for d in range(1, N_T):
        gc_copy(d).wait_send()
    gd_copy().wait_send()
    gf_copy().wait_send()


def copy_kernel(*refs):
    count = len(refs) // 2
    for i in range(count):
        refs[count + i][...] = refs[i][...]


def body(
    features,
    weight,
    cotangent,
    node_order,
    forward_tiles,
    forward_slots,
    forward_count,
    backward_tiles,
    backward_slots,
    backward_count,
):
    scale = 1.0 / math.sqrt(BLOCK * lax.axis_size("rows"))
    any_spec = pl.BlockSpec(memory_space=pl.ANY)
    dma = pltpu.SemaphoreType.DMA

    def kernel(*refs):
        layer_kernel(scale, *refs)

    results = pl.pallas_call(
        kernel,
        out_shape=[
            jax.ShapeDtypeStruct((BLOCK, FEAT), BF16),
            jax.ShapeDtypeStruct((FEAT, FEAT), F32),
            jax.ShapeDtypeStruct((BLOCK, FEAT), BF16),
        ],
        in_specs=[pl.BlockSpec(memory_space=pltpu.SMEM)] * 2 + [any_spec] * 8,
        out_specs=[any_spec] * 3,
        scratch_shapes=[
            pltpu.VMEM((2, N_T, 2, CAP), jnp.int32),
            pltpu.VMEM((2 * N_T, TILE), jnp.int32),
            pltpu.SMEM((2 * N_T, TILE), jnp.int32),
            pltpu.VMEM((1, BLOCK), jnp.int32),
            pltpu.VMEM((BLOCK, FEAT), BF16),
            pltpu.VMEM((FEAT, FEAT), BF16),
            pltpu.VMEM((BLOCK, FEAT), BF16),
            pltpu.VMEM((N_T, CAP + 1, TILE, TILE), BF16),
            pltpu.VMEM((N_T, CAP + 1, TILE, TILE), BF16),
            pltpu.VMEM((2, N_T, BLOCK, BLOCK), BF16),
            pltpu.VMEM((BLOCK, BLOCK), BF16),
            pltpu.VMEM((2, N_T, N_X, 2, SHARE, FEAT), BF16),
            pltpu.VMEM((2, SHARE, FEAT), BF16),
            pltpu.VMEM((2, N_Y, PART_A, FEAT), BF16),
            pltpu.VMEM((2, N_X, PART_A, FEAT), BF16),
            pltpu.VMEM((2, N_Y, N_T, PART_B, FEAT), BF16),
            pltpu.VMEM((BLOCK, FEAT), F32),
            pltpu.VMEM((2, BLOCK, FEAT), BF16),
            pltpu.VMEM((N_X, 2 * SHARE, FEAT), BF16),
            pltpu.VMEM((SHARE, FEAT), BF16),
            pltpu.VMEM((2 * SHARE, FEAT), F32),
            pltpu.VMEM((SHARE, FEAT), BF16),
            pltpu.VMEM((N_REP, SHARE, FEAT), BF16),
            pltpu.VMEM((2, SHARE, FEAT), BF16),
            pltpu.VMEM((FEAT, FEAT), F32),
            pltpu.VMEM((FEAT // 2, FEAT), F32),
            pltpu.VMEM((FEAT // 2, FEAT), F32),
            pltpu.VMEM((N_REP, GROWS, FEAT), F32),
            pltpu.VMEM((N_Y, GROWS, FEAT), F32),
            pltpu.VMEM((N_T, GROWS, FEAT), F32),
            pltpu.VMEM((FEAT // 2, FEAT), F32),
            dma((9,)),
            dma((2, N_Y)),
            dma((2, N_Y)),
            dma((2, N_Y)),
            dma((2, N_Y)),
            dma((2, N_Y)),
            dma((2, N_Y)),
            dma((2, N_Y)),
            dma((2, N_Y)),
            dma((2, N_T, N_Y)),
            dma((2, N_T, N_Y)),
            dma((2, N_T, N_Y)),
            dma((2, N_T, N_Y)),
            dma((2, N_T)),
            dma((2, N_T)),
            dma((N_X,)),
            dma((N_X,)),
            dma((1,)),
            dma((1,)),
            dma((N_X,)),
            dma((N_REP,)),
            dma((N_REP,)),
            dma((2, N_REP)),
            dma((2, N_REP)),
            dma((N_REP,)),
            dma((N_REP,)),
            dma((N_Y,)),
            dma((N_Y,)),
            dma((N_T,)),
            dma((N_T,)),
            dma((1,)),
            dma((1,)),
            dma((N_REP,)),
            dma((N_REP,)),
            dma((1,)),
            dma((1,)),
            dma((3,)),
        ],
        compiler_params=pltpu.CompilerParams(
            collective_id=0, has_side_effects=True, vmem_limit_bytes=56 * 1024 * 1024
        ),
    )(
        forward_count[0, 0],
        backward_count[0, 0],
        forward_slots[0, 0],
        backward_slots[0, 0],
        node_order,
        features,
        weight,
        cotangent,
        forward_tiles[0, 0],
        backward_tiles[0, 0],
    )
    return pl.pallas_call(
        copy_kernel,
        out_shape=[jax.ShapeDtypeStruct(r.shape, r.dtype) for r in results],
        in_specs=[pl.BlockSpec(memory_space=pltpu.VMEM)] * 3,
        out_specs=[pl.BlockSpec(memory_space=pltpu.VMEM)] * 3,
    )(*results)


def solution(mesh):
    placed = (
        P("rows", None),
        P(),
        P("rows", None),
        P("rows", None),
        P("rows", "rep", None, None, None, None),
        P("rows", "rep", None, None, None),
        P("rows", "rep", None),
        P("rows", "rep", None, None, None, None),
        P("rows", "rep", None, None, None),
        P("rows", "rep", None),
    )
    return jax.shard_map(
        body,
        mesh=mesh,
        in_specs=placed,
        out_specs=(P("rows", None), P(), P("rows", None)),
        check_vma=False,
    )
```

```python
import math

import jax
import jax.numpy as jnp
from jax import lax
from jax.experimental import pallas as pl
from jax.experimental.pallas import tpu as pltpu
from jax.sharding import PartitionSpec as P

F32 = jnp.float32
BF16 = jnp.bfloat16
MESH = pl.DeviceIdType.MESH

N_X = 4
N_Y = 4
N_T = 4
N_REP = 8
BLOCK = 1024
FEAT = 256
TILE = 128
GRID = BLOCK // TILE
CAP = 32
SHARE = BLOCK // N_REP
PART_A = (48, 48)
PART_B = tuple(SHARE - rows for rows in PART_A)
GROWS = FEAT // 2 // N_REP


def rows_index(t, y, core):
    return (t * N_Y + y) * 2 + core


def layer_kernel(
    scale,
    fcount_ref,
    bcount_ref,
    fslots_hbm,
    bslots_hbm,
    order_hbm,
    feat_hbm,
    weight_hbm,
    cot_hbm,
    ftiles_hbm,
    btiles_hbm,
    lo_ref,
    gw_ref,
    gi_ref,
    slots_v,
    map_v,
    map_ref,
    order_v,
    feat_v,
    weight_v,
    cot_v,
    ftiles_v,
    btiles_v,
    dense,
    unperm,
    src,
    own,
    ya_f,
    ya_b,
    xa_f,
    xa_b,
    yb_f,
    yb_b,
    part,
    part_b,
    rsx_land,
    rsz_land,
    rs_mid,
    rsz_out,
    rs_land,
    share_v,
    gterm,
    gd_land,
    gmid,
    ga_land,
    gb_land,
    gc_land,
    ghalf,
    local_sem,
    ya_send,
    ya_recv,
    xa_send,
    xa_recv,
    za_send,
    za_recv,
    zb_send,
    zb_recv,
    yb_send,
    yb_recv,
    xb_send,
    xb_recv,
    side_send,
    side_recv,
    rsx_send,
    rsx_recv,
    rsz_send,
    rsz_recv,
    agz_send,
    rs_send,
    rs_recv,
    ag_send,
    ag_recv,
    ga_send,
    ga_recv,
    gb_send,
    gb_recv,
    gc_send,
    gc_recv,
    gd_send,
    gd_recv,
    ge_send,
    ge_recv,
    gf_send,
    gf_recv,
    out_sem,
):
    me = lax.axis_index("rows")
    rep = lax.axis_index("rep")
    core = me % 2
    y = (me // 2) % N_Y
    t = me // (2 * N_Y)
    x = rep // 2
    zl = rep % 2
    other = 1 - core
    straight = core == zl
    crossed = jnp.logical_not(straight)
    blocks = [(t + d) % N_T for d in (0, 1, 3, 2)]

    sibling = (rows_index(t, y, other), rep)

    def y_peer(d):
        return (rows_index(t, (y + d) % N_Y, core), rep)

    def cross_peer(d):
        return (rows_index((t + d) % N_T, y, zl), x * 2 + core)

    def z_peer(d):
        return (rows_index((t + d) % N_T, y, core), rep)

    def rep_index(d):
        dx, dz = d // 2, d % 2
        px = (x + dx) % N_X
        pz = (zl + dz) % 2
        return px * 2 + pz

    def rep_from(d):
        dx, dz = d // 2, d % 2
        return ((x + N_X - dx) % N_X) * 2 + (zl + dz) % 2

    def rep_peer(d):
        return (me, rep_index(d))

    def remote(source_ref, target_ref, send, recv, device):
        return pltpu.make_async_remote_copy(
            src_ref=source_ref,
            dst_ref=target_ref,
            send_sem=send,
            recv_sem=recv,
            device_id=device,
            device_id_type=MESH,
        )

    loads = [
        pltpu.make_async_copy(order_hbm, order_v, local_sem.at[0]),
        pltpu.make_async_copy(feat_hbm, feat_v, local_sem.at[1]),
        pltpu.make_async_copy(weight_hbm, weight_v, local_sem.at[2]),
        pltpu.make_async_copy(cot_hbm, cot_v, local_sem.at[3]),
        pltpu.make_async_copy(ftiles_hbm, ftiles_v.at[:, pl.ds(0, CAP)], local_sem.at[4]),
        pltpu.make_async_copy(btiles_hbm, btiles_v.at[:, pl.ds(0, CAP)], local_sem.at[5]),
        pltpu.make_async_copy(fslots_hbm, slots_v.at[0], local_sem.at[6]),
        pltpu.make_async_copy(bslots_hbm, slots_v.at[1], local_sem.at[7]),
    ]
    tiles = (ftiles_v, btiles_v)
    for held in tiles:
        for s in range(N_T):
            held[s, CAP] = jnp.zeros((TILE, TILE), BF16)
    for load in loads:
        load.start()

    barrier = pltpu.get_barrier_semaphore()
    partners = [sibling]
    partners += [y_peer(d) for d in range(1, N_Y)]
    partners += [z_peer(d) for d in range(1, N_T)]
    partners += [cross_peer(d) for d in range(1, N_T)]
    partners += [rep_peer(d) for d in range(1, N_REP)]
    for partner in partners:
        pl.semaphore_signal(barrier, inc=1, device_id=partner, device_id_type=MESH)

    @pl.when(crossed)
    def _():
        pl.semaphore_signal(barrier, inc=1, device_id=cross_peer(0), device_id_type=MESH)

    def share_rows(index):
        return pl.ds(pl.multiple_of(index * SHARE, SHARE), SHARE)

    loads[0].wait()
    wanted = jnp.transpose(jnp.broadcast_to(order_v[0:1, share_rows(rep)], (SHARE, SHARE)))
    lanes = lax.broadcasted_iota(jnp.int32, (SHARE, TILE), 1)
    one_hot = jnp.concatenate(
        [jnp.where(wanted == lanes + b * TILE, 1.0, 0.0).astype(BF16) for b in range(GRID)], axis=1
    )
    loads[1].wait()
    own[0] = jnp.dot(one_hot, feat_v[...], preferred_element_type=F32).astype(BF16)
    ya_f[y] = own[0, 0 : PART_A[0], :]

    @pl.when(straight)
    def _():
        yb_f[y, t] = own[0, PART_A[0] : SHARE, :]
        pl.semaphore_wait(barrier, len(partners))

    @pl.when(crossed)
    def _():
        pl.semaphore_wait(barrier, len(partners) + 1)

    land_ya = (ya_f, ya_b)
    land_xa = (xa_f, xa_b)
    land_yb = (yb_f, yb_b)
    first_a = [pl.ds(0, rows) for rows in PART_A]
    last_b = [pl.ds(rows, SHARE - rows) for rows in PART_A]

    def ya_copy(p, d):
        ref = land_ya[p].at[y]
        return remote(ref, ref, ya_send.at[p, d], ya_recv.at[p, d], y_peer(d))

    def xa_copy(p, d):
        return remote(
            land_ya[p].at[(x + d) % N_X], land_xa[p].at[x], xa_send.at[p, d], xa_recv.at[p, d], rep_peer(2 * d)
        )

    def za_copy(p, d):
        return remote(
            land_xa[p],
            src.at[p, t, :, zl, first_a[p], :],
            za_send.at[p, d],
            za_recv.at[p, d],
            cross_peer(d),
        )

    def zb_copy(p, d):
        return remote(
            own.at[p, last_b[p], :], land_yb[p].at[y, t], zb_send.at[p, d], zb_recv.at[p, d], cross_peer(d)
        )

    def yb_copy(p, i, d):
        ref = land_yb[p].at[y, blocks[i]]
        return remote(ref, ref, yb_send.at[p, i, d], yb_recv.at[p, i, d], y_peer(d))

    def xb_copy(p, i, d):
        return remote(
            land_yb[p].at[(x + d) % N_X, blocks[i]],
            src.at[p, blocks[i], x, core, last_b[p], :],
            xb_send.at[p, i, d],
            xb_recv.at[p, i, d],
            rep_peer(2 * d),
        )

    def side_copy(p, i):
        ref = src.at[p, blocks[i], :, core]
        return remote(ref, ref, side_send.at[p, i], side_recv.at[p, i], sibling)

    from_z = (0, 3, 1, 2)

    def begin(p):
        for d in (2, 1, 3):
            zb_copy(p, d).start()

        @pl.when(crossed)
        def _():
            zb_copy(p, 0).start()

        for d in (2, 1, 3):
            ya_copy(p, d).start()

    def z_wait(copy, i):
        if i == 0:

            @pl.when(crossed)
            def _():
                copy.wait_recv()

        else:
            copy.wait_recv()

    def a_over_x(p):
        for d in (1, 2, 3):
            ya_copy(p, d).wait_recv()
        for d in (2, 1, 3):
            xa_copy(p, d).start()
        land_xa[p][x] = land_ya[p][x]

    def a_over_z(p):
        for d in (1, 2, 3):
            xa_copy(p, d).wait_recv()
        for d in (2, 1, 3):
            za_copy(p, d).start()

        @pl.when(crossed)
        def _():
            za_copy(p, 0).start()

        @pl.when(straight)
        def _():
            src[p, t, :, zl, first_a[p], :] = land_xa[p][...]

    def b_over_y(p):
        for i in range(N_T):
            z_wait(zb_copy(p, from_z[i]), i)
            for d in (2, 1, 3):
                yb_copy(p, i, d).start()

    def b_over_x(p):
        for i in range(N_T):
            for d in (1, 2, 3):
                yb_copy(p, i, d).wait_recv()
            for d in (2, 1, 3):
                xb_copy(p, i, d).start()
            src[p, blocks[i], x, core, last_b[p], :] = land_yb[p][x, blocks[i]]

    def finish(p, i):
        for d in (1, 2, 3):
            xb_copy(p, i, d).wait_recv()
        z_wait(za_copy(p, from_z[i]), i)
        side_copy(p, i).start()

    def use_all(p):
        part[...] = jnp.zeros((BLOCK, FEAT), F32)

        @pl.loop(0, N_T)
        def _(i):
            block = (t + i + i // 2 * (5 - 2 * i)) % N_T
            ref = src.at[p, block, :, core]
            remote(ref, ref, side_send.at[p, i], side_recv.at[p, i], sibling).wait_recv()
            part[...] += jnp.dot(
                dense[p, block], src[p, block].reshape(BLOCK, FEAT), preferred_element_type=F32
            )

    def slot_maps():
        loads[6].wait()
        loads[7].wait()
        count_refs = (fcount_ref, bcount_ref)
        rows8 = lax.broadcasted_iota(jnp.int32, (2 * N_T, 1), 0)
        live = jnp.zeros((2 * N_T, 1), jnp.int32)
        for row in range(2 * N_T):
            live = jnp.where(rows8 == row, count_refs[row // N_T][row % N_T], live)
        keys = jnp.concatenate(
            [slots_v[p, s, 0:1, :] * GRID + slots_v[p, s, 1:2, :] for p in range(2) for s in range(N_T)],
            axis=0,
        )
        cells = lax.broadcasted_iota(jnp.int32, (2 * N_T, TILE), 1)
        found = jnp.full((2 * N_T, TILE), CAP, jnp.int32)
        for slot in range(CAP):
            hit = jnp.logical_and(keys[:, slot : slot + 1] == cells, live > slot)
            found = jnp.where(hit, slot, found)
        map_v[...] = found
        to_scalar = pltpu.make_async_copy(map_v, map_ref, local_sem.at[8])
        to_scalar.start()
        to_scalar.wait()

    def lay_out(p):
        loads[4 + p].wait()

        @pl.loop(0, N_T * GRID)
        def _(step):
            s = step // GRID
            a = step % GRID
            rows = pl.ds(pl.multiple_of(a * TILE, TILE), TILE)
            for b in range(GRID):
                slot = map_ref[p * N_T + s, a * GRID + b]
                dense[p, s, rows, pl.ds(b * TILE, TILE)] = tiles[p][s, slot]

    begin(0)
    loads[2].wait()
    loads[3].wait()
    own[1] = lax.dot_general(
        cot_v[share_rows(rep), :], weight_v[...], (((1,), (1,)), ((), ())), preferred_element_type=F32
    ).astype(BF16)
    ya_b[y] = own[1, 0 : PART_A[1], :]

    @pl.when(straight)
    def _():
        yb_b[y, t] = own[1, PART_A[1] : SHARE, :]

    begin(1)
    slot_maps()
    a_over_x(0)
    b_over_y(0)
    a_over_z(0)
    lay_out(0)
    b_over_x(0)
    lay_out(1)

    @pl.loop(0, GRID)
    def _(a):
        rows = pl.ds(pl.multiple_of(a * TILE, TILE), TILE)
        spots = lax.broadcasted_iota(jnp.int32, (TILE, BLOCK), 0) + a * TILE
        unperm[rows, :] = jnp.where(order_v[...] == spots, 1.0, 0.0).astype(BF16)

    finish(0, 0)
    finish(0, 1)
    a_over_x(1)
    finish(0, 2)
    finish(0, 3)
    b_over_y(1)
    a_over_z(1)
    use_all(0)

    def pair_rows(index):
        return pl.ds(pl.multiple_of(index * 2 * SHARE, 2 * SHARE), 2 * SHARE)

    def rsx_copy(d):
        return remote(
            part_b.at[0, pair_rows((x + d) % N_X), :],
            rsx_land.at[d],
            rsx_send.at[d],
            rsx_recv.at[d],
            rep_peer(2 * d),
        )

    def rsz_copy():
        return remote(rsz_out, rsz_land, rsz_send.at[0], rsz_recv.at[0], rep_peer(1))

    part_b[0] = part[...].astype(BF16)
    for d in (2, 1, 3):
        rsx_copy(d).start()

    b_over_x(1)
    total = part[pair_rows(x), :]
    for d in range(1, N_X):
        rsx_copy(d).wait_recv()
        total = total + rsx_land[d].astype(F32)
    rs_mid[...] = total
    rsz_out[...] = rs_mid[share_rows(1 - zl), :].astype(BF16)
    rsz_copy().start()

    finish(1, 0)
    finish(1, 1)

    partner = rep_index(1)

    def ag_own(d):
        return remote(
            share_v.at[0], lo_ref.at[share_rows(rep), :], ag_send.at[0, d], ag_recv.at[0, d], rep_peer(d)
        )

    def ag_pass(d):
        rows = share_rows(partner)
        return remote(
            lo_ref.at[rows, :], lo_ref.at[rows, :], agz_send.at[d], ag_recv.at[0, 2 * d + 1], rep_peer(2 * d)
        )

    rsz_copy().wait_recv()
    agg = (rs_mid[share_rows(zl), :] + rsz_land[...].astype(F32)).astype(BF16)
    share_v[0] = jnp.dot(agg, weight_v[...], preferred_element_type=F32).astype(BF16)
    for d in (1, 4, 2, 6):
        ag_own(d).start()
    lo_own = pltpu.make_async_copy(share_v.at[0], lo_ref.at[share_rows(rep), :], out_sem.at[0])
    lo_own.start()

    gterm[...] = lax.dot_general(
        agg, cot_v[share_rows(rep), :], (((0,), (0,)), ((), ())), preferred_element_type=F32
    )
    ghalf_rows = FEAT // 2

    def core_rows(index):
        return pl.ds(pl.multiple_of(index * ghalf_rows, ghalf_rows), ghalf_rows)

    def gd_copy():
        return remote(
            gterm.at[core_rows(other), :], gd_land, gd_send.at[0], gd_recv.at[0], sibling
        )

    def g_rows(index):
        return pl.ds(pl.multiple_of(index * GROWS, GROWS), GROWS)

    def ga_copy(d):
        return remote(
            gmid.at[g_rows(rep_index(d)), :],
            ga_land.at[d],
            ga_send.at[d],
            ga_recv.at[d],
            rep_peer(d),
        )

    def gb_copy(d):
        return remote(gb_land.at[y], gb_land.at[y], gb_send.at[d], gb_recv.at[d], y_peer(d))

    def gc_copy(d):
        return remote(gc_land.at[t], gc_land.at[t], gc_send.at[d], gc_recv.at[d], z_peer(d))

    def ge_copy(d):
        mine = ghalf.at[g_rows(rep), :]
        return remote(mine, mine, ge_send.at[d], ge_recv.at[d], rep_peer(d))

    def gf_copy():
        return remote(
            ghalf, gw_ref.at[core_rows(core), :], gf_send.at[0], gf_recv.at[0], sibling
        )

    gd_copy().start()

    finish(1, 2)
    finish(1, 3)
    gd_copy().wait_recv()
    gmid[...] = gterm[core_rows(core), :] + gd_land[...]
    for d in range(1, N_REP):
        ga_copy(d).start()

    use_all(1)
    part_b[1] = part[...].astype(BF16)
    part[...] = jnp.dot(unperm[...], part_b[1], preferred_element_type=F32)
    part_b[1] = part[...].astype(BF16)

    def rs_copy(d):
        return remote(
            part_b.at[1, share_rows(rep_index(d)), :],
            rs_land.at[d],
            rs_send.at[d],
            rs_recv.at[d],
            rep_peer(d),
        )

    def ag_copy(d):
        return remote(
            share_v.at[1], gi_ref.at[share_rows(rep), :], ag_send.at[1, d], ag_recv.at[1, d], rep_peer(d)
        )

    far_first = (5, 4, 3, 7, 2, 6, 1)
    for d in far_first:
        rs_copy(d).start()

    ag_own(1).wait_recv()
    for d in range(1, N_X):
        ag_pass(d).start()

    gsum = gmid[g_rows(rep), :]
    for d in range(1, N_REP):
        ga_copy(d).wait_recv()
        gsum = gsum + ga_land[d]
    gb_land[y] = gsum
    for d in range(1, N_Y):
        gb_copy(d).start()
    for d in range(1, N_Y):
        gb_copy(d).wait_recv()
    gc_land[t] = gb_land[0] + gb_land[1] + gb_land[2] + gb_land[3]
    for d in range(1, N_T):
        gc_copy(d).start()
    for d in range(1, N_T):
        gc_copy(d).wait_recv()
    ghalf[g_rows(rep), :] = (gc_land[0] + gc_land[1] + gc_land[2] + gc_land[3]) * scale
    for d in range(1, N_REP):
        ge_copy(d).start()

    back_total = part[share_rows(rep), :]
    for d in range(1, N_REP):
        rs_copy(d).wait_recv()
        back_total = back_total + rs_land[d].astype(F32)
    keep = feat_v[share_rows(rep), :].astype(F32) > 0.0
    share_v[1] = jnp.where(keep, back_total, 0.0).astype(BF16)
    for d in far_first:
        ag_copy(d).start()
    gi_own = pltpu.make_async_copy(share_v.at[1], gi_ref.at[share_rows(rep), :], out_sem.at[1])
    gi_own.start()

    for d in range(1, N_REP):
        ge_copy(d).wait_recv()
    gf_copy().start()
    gw_own = pltpu.make_async_copy(ghalf, gw_ref.at[core_rows(core), :], out_sem.at[2])
    gw_own.start()

    for p in range(2):

        @pl.when(crossed)
        def _():
            zb_copy(p, 0).wait_send()
            za_copy(p, 0).wait_send()

        for d in (1, 2, 3):
            ya_copy(p, d).wait_send()
            xa_copy(p, d).wait_send()
            za_copy(p, d).wait_send()
            zb_copy(p, d).wait_send()
            for i in range(N_T):
                yb_copy(p, i, d).wait_send()
                xb_copy(p, i, d).wait_send()
        for i in range(N_T):
            side_copy(p, i).wait_send()
    for d in (1, 2, 4, 6):
        ag_own(d).wait_send()
    for d in range(1, N_X):
        rsx_copy(d).wait_send()
        ag_pass(d).wait_send()
    rsz_copy().wait_send()
    for d in range(1, N_REP):
        rs_copy(d).wait_send()
        ga_copy(d).wait_send()
    for d in range(1, N_Y):
        gb_copy(d).wait_send()
    for d in range(1, N_T):
        gc_copy(d).wait_send()
    gd_copy().wait_send()

    for d in (2, 4, 6, 3, 5, 7):
        ag_own(d).wait_recv()
    for d in range(1, N_REP):
        ag_copy(d).wait_recv()
    gf_copy().wait_recv()
    lo_own.wait()
    gi_own.wait()
    gw_own.wait()
    for d in range(1, N_REP):
        ag_copy(d).wait_send()
        ge_copy(d).wait_send()
    gf_copy().wait_send()

def copy_kernel(*refs):
    count = len(refs) // 2
    for i in range(count):
        refs[count + i][...] = refs[i][...]


def body(
    features,
    weight,
    cotangent,
    node_order,
    forward_tiles,
    forward_slots,
    forward_count,
    backward_tiles,
    backward_slots,
    backward_count,
):
    scale = 1.0 / math.sqrt(BLOCK * lax.axis_size("rows"))
    any_spec = pl.BlockSpec(memory_space=pl.ANY)
    dma = pltpu.SemaphoreType.DMA

    def kernel(*refs):
        layer_kernel(scale, *refs)

    results = pl.pallas_call(
        kernel,
        out_shape=[
            jax.ShapeDtypeStruct((BLOCK, FEAT), BF16),
            jax.ShapeDtypeStruct((FEAT, FEAT), F32),
            jax.ShapeDtypeStruct((BLOCK, FEAT), BF16),
        ],
        in_specs=[pl.BlockSpec(memory_space=pltpu.SMEM)] * 2 + [any_spec] * 8,
        out_specs=[any_spec] * 3,
        scratch_shapes=[
            pltpu.VMEM((2, N_T, 2, CAP), jnp.int32),
            pltpu.VMEM((2 * N_T, TILE), jnp.int32),
            pltpu.SMEM((2 * N_T, TILE), jnp.int32),
            pltpu.VMEM((1, BLOCK), jnp.int32),
            pltpu.VMEM((BLOCK, FEAT), BF16),
            pltpu.VMEM((FEAT, FEAT), BF16),
            pltpu.VMEM((BLOCK, FEAT), BF16),
            pltpu.VMEM((N_T, CAP + 1, TILE, TILE), BF16),
            pltpu.VMEM((N_T, CAP + 1, TILE, TILE), BF16),
            pltpu.VMEM((2, N_T, BLOCK, BLOCK), BF16),
            pltpu.VMEM((BLOCK, BLOCK), BF16),
            pltpu.VMEM((2, N_T, N_X, 2, SHARE, FEAT), BF16),
            pltpu.VMEM((2, SHARE, FEAT), BF16),
            pltpu.VMEM((N_Y, PART_A[0], FEAT), BF16),
            pltpu.VMEM((N_Y, PART_A[1], FEAT), BF16),
            pltpu.VMEM((N_X, PART_A[0], FEAT), BF16),
            pltpu.VMEM((N_X, PART_A[1], FEAT), BF16),
            pltpu.VMEM((N_Y, N_T, PART_B[0], FEAT), BF16),
            pltpu.VMEM((N_Y, N_T, PART_B[1], FEAT), BF16),
            pltpu.VMEM((BLOCK, FEAT), F32),
            pltpu.VMEM((2, BLOCK, FEAT), BF16),
            pltpu.VMEM((N_X, 2 * SHARE, FEAT), BF16),
            pltpu.VMEM((SHARE, FEAT), BF16),
            pltpu.VMEM((2 * SHARE, FEAT), F32),
            pltpu.VMEM((SHARE, FEAT), BF16),
            pltpu.VMEM((N_REP, SHARE, FEAT), BF16),
            pltpu.VMEM((2, SHARE, FEAT), BF16),
            pltpu.VMEM((FEAT, FEAT), F32),
            pltpu.VMEM((FEAT // 2, FEAT), F32),
            pltpu.VMEM((FEAT // 2, FEAT), F32),
            pltpu.VMEM((N_REP, GROWS, FEAT), F32),
            pltpu.VMEM((N_Y, GROWS, FEAT), F32),
            pltpu.VMEM((N_T, GROWS, FEAT), F32),
            pltpu.VMEM((FEAT // 2, FEAT), F32),
            dma((9,)),
            dma((2, N_Y)),
            dma((2, N_Y)),
            dma((2, N_Y)),
            dma((2, N_Y)),
            dma((2, N_Y)),
            dma((2, N_Y)),
            dma((2, N_Y)),
            dma((2, N_Y)),
            dma((2, N_T, N_Y)),
            dma((2, N_T, N_Y)),
            dma((2, N_T, N_Y)),
            dma((2, N_T, N_Y)),
            dma((2, N_T)),
            dma((2, N_T)),
            dma((N_X,)),
            dma((N_X,)),
            dma((1,)),
            dma((1,)),
            dma((N_X,)),
            dma((N_REP,)),
            dma((N_REP,)),
            dma((2, N_REP)),
            dma((2, N_REP)),
            dma((N_REP,)),
            dma((N_REP,)),
            dma((N_Y,)),
            dma((N_Y,)),
            dma((N_T,)),
            dma((N_T,)),
            dma((1,)),
            dma((1,)),
            dma((N_REP,)),
            dma((N_REP,)),
            dma((1,)),
            dma((1,)),
            dma((3,)),
        ],
        compiler_params=pltpu.CompilerParams(
            collective_id=0, has_side_effects=True, vmem_limit_bytes=56 * 1024 * 1024
        ),
    )(
        forward_count[0, 0],
        backward_count[0, 0],
        forward_slots[0, 0],
        backward_slots[0, 0],
        node_order,
        features,
        weight,
        cotangent,
        forward_tiles[0, 0],
        backward_tiles[0, 0],
    )
    return pl.pallas_call(
        copy_kernel,
        out_shape=[jax.ShapeDtypeStruct(r.shape, r.dtype) for r in results],
        in_specs=[pl.BlockSpec(memory_space=pltpu.VMEM)] * 3,
        out_specs=[pl.BlockSpec(memory_space=pltpu.VMEM)] * 3,
    )(*results)


def solution(mesh):
    placed = (
        P("rows", None),
        P(),
        P("rows", None),
        P("rows", None),
        P("rows", "rep", None, None, None, None),
        P("rows", "rep", None, None, None),
        P("rows", "rep", None),
        P("rows", "rep", None, None, None, None),
        P("rows", "rep", None, None, None),
        P("rows", "rep", None),
    )
    return jax.shard_map(
        body,
        mesh=mesh,
        in_specs=placed,
        out_specs=(P("rows", None), P(), P("rows", None)),
        check_vma=False,
    )
```

```python
import math

import jax
import jax.numpy as jnp
from jax import lax
from jax.experimental import pallas as pl
from jax.experimental.pallas import tpu as pltpu
from jax.sharding import PartitionSpec as P

F32 = jnp.float32
BF16 = jnp.bfloat16
MESH = pl.DeviceIdType.MESH

N_X = 4
N_Y = 4
N_T = 4
N_REP = 8
BLOCK = 1024
FEAT = 256
TILE = 128
GRID = BLOCK // TILE
CAP = 32
SHARE = BLOCK // N_REP
PIECES = 2
PART_A = (48, 48)
PART_B = tuple(SHARE - rows for rows in PART_A)
GROWS = FEAT // 2 // N_REP


def rows_index(t, y, core):
    return (t * N_Y + y) * 2 + core


def layer_kernel(
    scale,
    fcount_ref,
    bcount_ref,
    fslots_hbm,
    bslots_hbm,
    order_hbm,
    feat_hbm,
    weight_hbm,
    cot_hbm,
    ftiles_hbm,
    btiles_hbm,
    lo_ref,
    gw_ref,
    gi_ref,
    slots_v,
    map_v,
    map_ref,
    order_v,
    feat_v,
    weight_v,
    cot_v,
    ftiles_v,
    btiles_v,
    dense,
    unperm,
    src,
    own,
    ya_f,
    ya_b,
    xa_f,
    xa_b,
    yb_f,
    yb_b,
    part,
    part_b,
    rsx_land,
    rsz_land,
    rs_mid,
    rsz_out,
    rs_land,
    share_v,
    gterm,
    gd_land,
    gmid,
    ga_land,
    gb_land,
    gc_land,
    ghalf,
    local_sem,
    ya_send,
    ya_recv,
    xa_send,
    xa_recv,
    za_send,
    za_recv,
    zb_send,
    zb_recv,
    yb_send,
    yb_recv,
    xb_send,
    xb_recv,
    side_send,
    side_recv,
    rsx_send,
    rsx_recv,
    rsz_send,
    rsz_recv,
    agz_send,
    rs_send,
    rs_recv,
    ag_send,
    ag_recv,
    ga_send,
    ga_recv,
    gb_send,
    gb_recv,
    gc_send,
    gc_recv,
    gd_send,
    gd_recv,
    ge_send,
    ge_recv,
    gf_send,
    gf_recv,
    out_sem,
):
    me = lax.axis_index("rows")
    rep = lax.axis_index("rep")
    core = lax.rem(me, 2)
    y = lax.rem(lax.div(me, 2), N_Y)
    t = lax.div(me, 2 * N_Y)
    x = lax.div(rep, 2)
    zl = lax.rem(rep, 2)
    other = 1 - core
    straight = core == zl
    crossed = jnp.logical_not(straight)
    blocks = [lax.rem(t + d, N_T) for d in (0, 1, 3, 2)]

    sibling = (rows_index(t, y, other), rep)

    def y_peer(d):
        return (rows_index(t, lax.rem(y + d, N_Y), core), rep)

    def cross_peer(d):
        return (rows_index(lax.rem(t + d, N_T), y, zl), x * 2 + core)

    def z_peer(d):
        return (rows_index(lax.rem(t + d, N_T), y, core), rep)

    def rep_index(d):
        dx, dz = d // 2, d % 2
        px = lax.rem(x + dx, N_X)
        pz = lax.rem(zl + dz, 2)
        return px * 2 + pz

    def rep_from(d):
        dx, dz = d // 2, d % 2
        return (lax.rem(x + N_X - dx, N_X)) * 2 + lax.rem(zl + dz, 2)

    def rep_peer(d):
        return (me, rep_index(d))

    def remote(source_ref, target_ref, send, recv, device):
        return pltpu.make_async_remote_copy(
            src_ref=source_ref,
            dst_ref=target_ref,
            send_sem=send,
            recv_sem=recv,
            device_id=device,
            device_id_type=MESH,
        )

    loads = [
        pltpu.make_async_copy(order_hbm, order_v, local_sem.at[0]),
        pltpu.make_async_copy(feat_hbm, feat_v, local_sem.at[1]),
        pltpu.make_async_copy(weight_hbm, weight_v, local_sem.at[2]),
        pltpu.make_async_copy(cot_hbm, cot_v, local_sem.at[3]),
        pltpu.make_async_copy(ftiles_hbm, ftiles_v.at[:, pl.ds(0, CAP)], local_sem.at[4]),
        pltpu.make_async_copy(btiles_hbm, btiles_v.at[:, pl.ds(0, CAP)], local_sem.at[5]),
        pltpu.make_async_copy(fslots_hbm, slots_v.at[0], local_sem.at[6]),
        pltpu.make_async_copy(bslots_hbm, slots_v.at[1], local_sem.at[7]),
    ]
    tiles = (ftiles_v, btiles_v)
    for held in tiles:
        for s in range(N_T):
            held[s, CAP] = jnp.zeros((TILE, TILE), BF16)
    for load in loads[:4] + loads[6:]:
        load.start()

    barrier = pltpu.get_barrier_semaphore()
    partners = [sibling]
    partners += [y_peer(d) for d in range(1, N_Y)]
    partners += [z_peer(d) for d in range(1, N_T)]
    partners += [cross_peer(d) for d in range(1, N_T)]
    partners += [rep_peer(d) for d in range(1, N_REP)]
    for partner in partners:
        pl.semaphore_signal(barrier, inc=1, device_id=partner, device_id_type=MESH)

    @pl.when(crossed)
    def _():
        pl.semaphore_signal(barrier, inc=1, device_id=cross_peer(0), device_id_type=MESH)

    def share_rows(index):
        return pl.ds(pl.multiple_of(index * SHARE, SHARE), SHARE)

    loads[0].wait()
    wanted = jnp.transpose(jnp.broadcast_to(order_v[0:1, share_rows(rep)], (SHARE, SHARE)))
    lanes = lax.broadcasted_iota(jnp.int32, (SHARE, TILE), 1)
    one_hot = jnp.concatenate(
        [jnp.where(wanted == lanes + b * TILE, 1.0, 0.0).astype(BF16) for b in range(GRID)], axis=1
    )
    loads[1].wait()
    own[0] = jnp.dot(one_hot, feat_v[...], preferred_element_type=F32).astype(BF16)
    ya_f[y] = own[0, 0 : PART_A[0], :]

    @pl.when(straight)
    def _():
        yb_f[y, t] = own[0, PART_A[0] : SHARE, :]
        pl.semaphore_wait(barrier, len(partners))

    @pl.when(crossed)
    def _():
        pl.semaphore_wait(barrier, len(partners) + 1)

    land_ya = (ya_f, ya_b)
    land_xa = (xa_f, xa_b)
    land_yb = (yb_f, yb_b)
    first_a = [pl.ds(0, rows) for rows in PART_A]
    last_b = [pl.ds(rows, SHARE - rows) for rows in PART_A]

    def ya_copy(p, d):
        ref = land_ya[p].at[y]
        return remote(ref, ref, ya_send.at[p, d], ya_recv.at[p, d], y_peer(d))

    def xa_copy(p, d):
        return remote(
            land_ya[p].at[lax.rem(x + d, N_X)], land_xa[p].at[x], xa_send.at[p, d], xa_recv.at[p, d], rep_peer(2 * d)
        )

    def za_copy(p, d):
        return remote(
            land_xa[p],
            src.at[p, t, :, zl, first_a[p], :],
            za_send.at[p, d],
            za_recv.at[p, d],
            cross_peer(d),
        )

    def zb_copy(p, d):
        return remote(
            own.at[p, last_b[p], :], land_yb[p].at[y, t], zb_send.at[p, d], zb_recv.at[p, d], cross_peer(d)
        )

    def yb_copy(p, i, d):
        ref = land_yb[p].at[y, blocks[i]]
        return remote(ref, ref, yb_send.at[p, i, d], yb_recv.at[p, i, d], y_peer(d))

    def xb_copy(p, i, d):
        return remote(
            land_yb[p].at[lax.rem(x + d, N_X), blocks[i]],
            src.at[p, blocks[i], x, core, last_b[p], :],
            xb_send.at[p, i, d],
            xb_recv.at[p, i, d],
            rep_peer(2 * d),
        )

    def side_copy(p, i):
        ref = src.at[p, blocks[i], :, core]
        return remote(ref, ref, side_send.at[p, i], side_recv.at[p, i], sibling)

    from_z = (0, 3, 1, 2)

    def begin(p):
        for d in (2, 1, 3):
            zb_copy(p, d).start()

        @pl.when(crossed)
        def _():
            zb_copy(p, 0).start()

        for d in (2, 1, 3):
            ya_copy(p, d).start()

    def z_wait(copy, i):
        if i == 0:

            @pl.when(crossed)
            def _():
                copy.wait_recv()

        else:
            copy.wait_recv()

    def a_over_x(p):
        for d in (1, 2, 3):
            ya_copy(p, d).wait_recv()
        for d in (2, 1, 3):
            xa_copy(p, d).start()
        land_xa[p][x] = land_ya[p][x]

    def a_over_z(p):
        for d in (1, 2, 3):
            xa_copy(p, d).wait_recv()
        for d in (2, 1, 3):
            za_copy(p, d).start()

        @pl.when(crossed)
        def _():
            za_copy(p, 0).start()

        @pl.when(straight)
        def _():
            src[p, t, :, zl, first_a[p], :] = land_xa[p][...]

    def b_over_y(p):
        for i in range(N_T):
            z_wait(zb_copy(p, from_z[i]), i)
            for d in (2, 1, 3):
                yb_copy(p, i, d).start()

    def b_over_x(p):
        for i in range(N_T):
            for d in (1, 2, 3):
                yb_copy(p, i, d).wait_recv()
            for d in (2, 1, 3):
                xb_copy(p, i, d).start()
            src[p, blocks[i], x, core, last_b[p], :] = land_yb[p][x, blocks[i]]

    def finish(p, i):
        for d in (1, 2, 3):
            xb_copy(p, i, d).wait_recv()
        z_wait(za_copy(p, from_z[i]), i)
        side_copy(p, i).start()

    def use_all(p):
        part[...] = jnp.zeros((BLOCK, FEAT), F32)

        @pl.loop(0, N_T)
        def _(i):
            block = lax.rem(t + i + i // 2 * (5 - 2 * i), N_T)
            ref = src.at[p, block, :, core]
            remote(ref, ref, side_send.at[p, i], side_recv.at[p, i], sibling).wait_recv()
            part[...] += jnp.dot(
                dense[p, block], src[p, block].reshape(BLOCK, FEAT), preferred_element_type=F32
            )

    def slot_maps():
        loads[6].wait()
        loads[7].wait()
        count_refs = (fcount_ref, bcount_ref)
        rows8 = lax.broadcasted_iota(jnp.int32, (2 * N_T, 1), 0)
        live = jnp.zeros((2 * N_T, 1), jnp.int32)
        for row in range(2 * N_T):
            live = jnp.where(rows8 == row, count_refs[row // N_T][row % N_T], live)
        keys = jnp.concatenate(
            [slots_v[p, s, 0:1, :] * GRID + slots_v[p, s, 1:2, :] for p in range(2) for s in range(N_T)],
            axis=0,
        )
        cells = lax.broadcasted_iota(jnp.int32, (2 * N_T, TILE), 1)
        found = jnp.full((2 * N_T, TILE), CAP, jnp.int32)
        for slot in range(CAP):
            hit = jnp.logical_and(keys[:, slot : slot + 1] == cells, live > slot)
            found = jnp.where(hit, slot, found)
        map_v[...] = found
        to_scalar = pltpu.make_async_copy(map_v, map_ref, local_sem.at[8])
        to_scalar.start()
        to_scalar.wait()

    def lay_out(p):
        loads[4 + p].wait()

        @pl.loop(0, N_T * GRID)
        def _(step):
            s = step // GRID
            a = step % GRID
            rows = pl.ds(pl.multiple_of(a * TILE, TILE), TILE)
            for b in range(GRID):
                slot = map_ref[p * N_T + s, a * GRID + b]
                dense[p, s, rows, pl.ds(b * TILE, TILE)] = tiles[p][s, slot]

    begin(0)
    loads[4].start()
    loads[5].start()
    loads[2].wait()
    loads[3].wait()
    own[1] = lax.dot_general(
        cot_v[share_rows(rep), :], weight_v[...], (((1,), (1,)), ((), ())), preferred_element_type=F32
    ).astype(BF16)
    ya_b[y] = own[1, 0 : PART_A[1], :]

    @pl.when(straight)
    def _():
        yb_b[y, t] = own[1, PART_A[1] : SHARE, :]

    begin(1)
    slot_maps()
    a_over_x(0)
    b_over_y(0)
    a_over_z(0)
    lay_out(0)
    b_over_x(0)
    lay_out(1)

    @pl.loop(0, GRID)
    def _(a):
        rows = pl.ds(pl.multiple_of(a * TILE, TILE), TILE)
        spots = lax.broadcasted_iota(jnp.int32, (TILE, BLOCK), 0) + a * TILE
        unperm[rows, :] = jnp.where(order_v[...] == spots, 1.0, 0.0).astype(BF16)

    finish(0, 0)
    finish(0, 1)
    a_over_x(1)
    finish(0, 2)
    finish(0, 3)
    b_over_y(1)
    a_over_z(1)
    use_all(0)

    def pair_rows(index):
        return pl.ds(pl.multiple_of(index * 2 * SHARE, 2 * SHARE), 2 * SHARE)

    def rsx_copy(d):
        return remote(
            part_b.at[0, pair_rows(lax.rem(x + d, N_X)), :],
            rsx_land.at[d],
            rsx_send.at[d],
            rsx_recv.at[d],
            rep_peer(2 * d),
        )

    def rsz_copy():
        return remote(rsz_out, rsz_land, rsz_send.at[0], rsz_recv.at[0], rep_peer(1))

    part_b[0] = part[...].astype(BF16)
    for d in (2, 1, 3):
        rsx_copy(d).start()

    b_over_x(1)
    total = part[pair_rows(x), :]
    for d in range(1, N_X):
        rsx_copy(d).wait_recv()
        total = total + rsx_land[d].astype(F32)
    rs_mid[...] = total
    rsz_out[...] = rs_mid[share_rows(1 - zl), :].astype(BF16)
    rsz_copy().start()

    finish(1, 0)
    finish(1, 1)

    partner = rep_index(1)

    def ag_own(d):
        return remote(
            share_v.at[0], lo_ref.at[share_rows(rep), :], ag_send.at[0, d], ag_recv.at[0, d], rep_peer(d)
        )

    def ag_pass(d):
        rows = share_rows(partner)
        return remote(
            lo_ref.at[rows, :], lo_ref.at[rows, :], agz_send.at[d], ag_recv.at[0, 2 * d + 1], rep_peer(2 * d)
        )

    rsz_copy().wait_recv()
    agg = (rs_mid[share_rows(zl), :] + rsz_land[...].astype(F32)).astype(BF16)
    share_v[0] = jnp.dot(agg, weight_v[...], preferred_element_type=F32).astype(BF16)
    for d in (1, 4, 2, 6):
        ag_own(d).start()
    lo_own = pltpu.make_async_copy(share_v.at[0], lo_ref.at[share_rows(rep), :], out_sem.at[0])
    lo_own.start()

    gterm[...] = lax.dot_general(
        agg, cot_v[share_rows(rep), :], (((0,), (0,)), ((), ())), preferred_element_type=F32
    )
    ghalf_rows = FEAT // 2

    def core_rows(index):
        return pl.ds(pl.multiple_of(index * ghalf_rows, ghalf_rows), ghalf_rows)

    def gd_copy():
        return remote(
            gterm.at[core_rows(other), :], gd_land, gd_send.at[0], gd_recv.at[0], sibling
        )

    def g_rows(index):
        return pl.ds(pl.multiple_of(index * GROWS, GROWS), GROWS)

    def ga_copy(d):
        return remote(
            gmid.at[g_rows(rep_index(d)), :],
            ga_land.at[d],
            ga_send.at[d],
            ga_recv.at[d],
            rep_peer(d),
        )

    def gb_copy(d):
        return remote(gb_land.at[y], gb_land.at[y], gb_send.at[d], gb_recv.at[d], y_peer(d))

    def gc_copy(d):
        return remote(gc_land.at[t], gc_land.at[t], gc_send.at[d], gc_recv.at[d], z_peer(d))

    def ge_copy(d):
        mine = ghalf.at[g_rows(rep), :]
        return remote(mine, mine, ge_send.at[d], ge_recv.at[d], rep_peer(d))

    def gf_copy():
        return remote(
            ghalf, gw_ref.at[core_rows(core), :], gf_send.at[0], gf_recv.at[0], sibling
        )

    gd_copy().start()

    finish(1, 2)
    finish(1, 3)
    gd_copy().wait_recv()
    gmid[...] = gterm[core_rows(core), :] + gd_land[...]
    for d in range(1, N_REP):
        ga_copy(d).start()

    use_all(1)
    part_b[1] = part[...].astype(BF16)
    part[...] = jnp.dot(unperm[...], part_b[1], preferred_element_type=F32)
    part_b[1] = part[...].astype(BF16)

    piece = SHARE // PIECES

    def piece_rows(index, h):
        return pl.ds(pl.multiple_of(index * SHARE + h * piece, piece), piece)

    def rs_copy(d, h):
        return remote(
            part_b.at[1, piece_rows(rep_index(d), h), :],
            rs_land.at[d, pl.ds(h * piece, piece)],
            rs_send.at[h, d],
            rs_recv.at[h, d],
            rep_peer(d),
        )

    def ag_copy(d, h):
        return remote(
            share_v.at[1, pl.ds(h * piece, piece)],
            gi_ref.at[piece_rows(rep, h), :],
            ag_send.at[1 + h, d],
            ag_recv.at[1 + h, d],
            rep_peer(d),
        )

    far_first = (5, 4, 3, 7, 2, 6, 1)
    for h in range(PIECES):
        for d in far_first:
            rs_copy(d, h).start()

    ag_own(1).wait_recv()
    for d in range(1, N_X):
        ag_pass(d).start()

    gsum = gmid[g_rows(rep), :]
    for d in range(1, N_REP):
        ga_copy(d).wait_recv()
        gsum = gsum + ga_land[d]
    gb_land[y] = gsum
    for d in range(1, N_Y):
        gb_copy(d).start()
    for d in range(1, N_Y):
        gb_copy(d).wait_recv()
    gc_land[t] = gb_land[0] + gb_land[1] + gb_land[2] + gb_land[3]
    for d in range(1, N_T):
        gc_copy(d).start()
    for d in range(1, N_T):
        gc_copy(d).wait_recv()
    ghalf[g_rows(rep), :] = (gc_land[0] + gc_land[1] + gc_land[2] + gc_land[3]) * scale
    for d in range(1, N_REP):
        ge_copy(d).start()

    for h in range(PIECES):
        back_total = part[piece_rows(rep, h), :]
        for d in range(1, N_REP):
            rs_copy(d, h).wait_recv()
            back_total = back_total + rs_land[d, h * piece : (h + 1) * piece].astype(F32)
        keep = feat_v[piece_rows(rep, h), :].astype(F32) > 0.0
        share_v[1, h * piece : (h + 1) * piece] = jnp.where(keep, back_total, 0.0).astype(BF16)
        for d in far_first:
            ag_copy(d, h).start()
    gi_own = pltpu.make_async_copy(share_v.at[1], gi_ref.at[share_rows(rep), :], out_sem.at[1])
    gi_own.start()

    for d in range(1, N_REP):
        ge_copy(d).wait_recv()
    gf_copy().start()
    gw_own = pltpu.make_async_copy(ghalf, gw_ref.at[core_rows(core), :], out_sem.at[2])
    gw_own.start()

    for p in range(2):

        @pl.when(crossed)
        def _():
            zb_copy(p, 0).wait_send()
            za_copy(p, 0).wait_send()

        for d in (1, 2, 3):
            ya_copy(p, d).wait_send()
            xa_copy(p, d).wait_send()
            za_copy(p, d).wait_send()
            zb_copy(p, d).wait_send()
            for i in range(N_T):
                yb_copy(p, i, d).wait_send()
                xb_copy(p, i, d).wait_send()
        for i in range(N_T):
            side_copy(p, i).wait_send()
    for d in (1, 2, 4, 6):
        ag_own(d).wait_send()
    for d in range(1, N_X):
        rsx_copy(d).wait_send()
        ag_pass(d).wait_send()
    rsz_copy().wait_send()
    for d in range(1, N_REP):
        for h in range(PIECES):
            rs_copy(d, h).wait_send()
        ga_copy(d).wait_send()
    for d in range(1, N_Y):
        gb_copy(d).wait_send()
    for d in range(1, N_T):
        gc_copy(d).wait_send()
    gd_copy().wait_send()

    for d in (2, 4, 6, 3, 5, 7):
        ag_own(d).wait_recv()
    for d in range(1, N_REP):
        for h in range(PIECES):
            ag_copy(d, h).wait_recv()
    gf_copy().wait_recv()
    lo_own.wait()
    gi_own.wait()
    gw_own.wait()
    for d in range(1, N_REP):
        for h in range(PIECES):
            ag_copy(d, h).wait_send()
        ge_copy(d).wait_send()
    gf_copy().wait_send()

def copy_kernel(*refs):
    sources, targets, held, sems = refs[:3], refs[3:6], refs[6:9], refs[9]
    pieces = []
    for n in range(3):
        rows = sources[n].shape[0] // 4
        for c in range(4):
            part = pl.ds(c * rows, rows)
            sem = sems.at[n * 4 + c]
            inward = pltpu.make_async_copy(sources[n].at[part], held[n].at[part], sem)
            inward.start()
            pieces.append((inward, pltpu.make_async_copy(held[n].at[part], targets[n].at[part], sem)))
    for inward, outward in pieces:
        inward.wait()
        outward.start()
    for _, outward in pieces:
        outward.wait()


def body(
    features,
    weight,
    cotangent,
    node_order,
    forward_tiles,
    forward_slots,
    forward_count,
    backward_tiles,
    backward_slots,
    backward_count,
):
    scale = 1.0 / math.sqrt(BLOCK * lax.axis_size("rows"))
    any_spec = pl.BlockSpec(memory_space=pl.ANY)
    dma = pltpu.SemaphoreType.DMA

    def kernel(*refs):
        layer_kernel(scale, *refs)

    results = pl.pallas_call(
        kernel,
        out_shape=[
            jax.ShapeDtypeStruct((BLOCK, FEAT), BF16),
            jax.ShapeDtypeStruct((FEAT, FEAT), F32),
            jax.ShapeDtypeStruct((BLOCK, FEAT), BF16),
        ],
        in_specs=[pl.BlockSpec(memory_space=pltpu.SMEM)] * 2 + [any_spec] * 8,
        out_specs=[any_spec] * 3,
        scratch_shapes=[
            pltpu.VMEM((2, N_T, 2, CAP), jnp.int32),
            pltpu.VMEM((2 * N_T, TILE), jnp.int32),
            pltpu.SMEM((2 * N_T, TILE), jnp.int32),
            pltpu.VMEM((1, BLOCK), jnp.int32),
            pltpu.VMEM((BLOCK, FEAT), BF16),
            pltpu.VMEM((FEAT, FEAT), BF16),
            pltpu.VMEM((BLOCK, FEAT), BF16),
            pltpu.VMEM((N_T, CAP + 1, TILE, TILE), BF16),
            pltpu.VMEM((N_T, CAP + 1, TILE, TILE), BF16),
            pltpu.VMEM((2, N_T, BLOCK, BLOCK), BF16),
            pltpu.VMEM((BLOCK, BLOCK), BF16),
            pltpu.VMEM((2, N_T, N_X, 2, SHARE, FEAT), BF16),
            pltpu.VMEM((2, SHARE, FEAT), BF16),
            pltpu.VMEM((N_Y, PART_A[0], FEAT), BF16),
            pltpu.VMEM((N_Y, PART_A[1], FEAT), BF16),
            pltpu.VMEM((N_X, PART_A[0], FEAT), BF16),
            pltpu.VMEM((N_X, PART_A[1], FEAT), BF16),
            pltpu.VMEM((N_Y, N_T, PART_B[0], FEAT), BF16),
            pltpu.VMEM((N_Y, N_T, PART_B[1], FEAT), BF16),
            pltpu.VMEM((BLOCK, FEAT), F32),
            pltpu.VMEM((2, BLOCK, FEAT), BF16),
            pltpu.VMEM((N_X, 2 * SHARE, FEAT), BF16),
            pltpu.VMEM((SHARE, FEAT), BF16),
            pltpu.VMEM((2 * SHARE, FEAT), F32),
            pltpu.VMEM((SHARE, FEAT), BF16),
            pltpu.VMEM((N_REP, SHARE, FEAT), BF16),
            pltpu.VMEM((2, SHARE, FEAT), BF16),
            pltpu.VMEM((FEAT, FEAT), F32),
            pltpu.VMEM((FEAT // 2, FEAT), F32),
            pltpu.VMEM((FEAT // 2, FEAT), F32),
            pltpu.VMEM((N_REP, GROWS, FEAT), F32),
            pltpu.VMEM((N_Y, GROWS, FEAT), F32),
            pltpu.VMEM((N_T, GROWS, FEAT), F32),
            pltpu.VMEM((FEAT // 2, FEAT), F32),
            dma((9,)),
            dma((2, N_Y)),
            dma((2, N_Y)),
            dma((2, N_Y)),
            dma((2, N_Y)),
            dma((2, N_Y)),
            dma((2, N_Y)),
            dma((2, N_Y)),
            dma((2, N_Y)),
            dma((2, N_T, N_Y)),
            dma((2, N_T, N_Y)),
            dma((2, N_T, N_Y)),
            dma((2, N_T, N_Y)),
            dma((2, N_T)),
            dma((2, N_T)),
            dma((N_X,)),
            dma((N_X,)),
            dma((1,)),
            dma((1,)),
            dma((N_X,)),
            dma((PIECES, N_REP)),
            dma((PIECES, N_REP)),
            dma((1 + PIECES, N_REP)),
            dma((1 + PIECES, N_REP)),
            dma((N_REP,)),
            dma((N_REP,)),
            dma((N_Y,)),
            dma((N_Y,)),
            dma((N_T,)),
            dma((N_T,)),
            dma((1,)),
            dma((1,)),
            dma((N_REP,)),
            dma((N_REP,)),
            dma((1,)),
            dma((1,)),
            dma((3,)),
        ],
        compiler_params=pltpu.CompilerParams(
            collective_id=0, has_side_effects=True, vmem_limit_bytes=56 * 1024 * 1024
        ),
    )(
        forward_count[0, 0],
        backward_count[0, 0],
        forward_slots[0, 0],
        backward_slots[0, 0],
        node_order,
        features,
        weight,
        cotangent,
        forward_tiles[0, 0],
        backward_tiles[0, 0],
    )
    return pl.pallas_call(
        copy_kernel,
        out_shape=[jax.ShapeDtypeStruct(r.shape, r.dtype) for r in results],
        in_specs=[any_spec] * 3,
        out_specs=[any_spec] * 3,
        scratch_shapes=[pltpu.VMEM(r.shape, r.dtype) for r in results] + [dma((12,))],
        compiler_params=pltpu.CompilerParams(vmem_limit_bytes=56 * 1024 * 1024),
    )(*results)


def solution(mesh):
    placed = (
        P("rows", None),
        P(),
        P("rows", None),
        P("rows", None),
        P("rows", "rep", None, None, None, None),
        P("rows", "rep", None, None, None),
        P("rows", "rep", None),
        P("rows", "rep", None, None, None, None),
        P("rows", "rep", None, None, None),
        P("rows", "rep", None),
    )
    return jax.shard_map(
        body,
        mesh=mesh,
        in_specs=placed,
        out_specs=(P("rows", None), P(), P("rows", None)),
        check_vma=False,
    )
```

```python
import math

import jax
import jax.numpy as jnp
from jax import lax
from jax.experimental import pallas as pl
from jax.experimental.pallas import tpu as pltpu
from jax.sharding import PartitionSpec as P

F32 = jnp.float32
BF16 = jnp.bfloat16
MESH = pl.DeviceIdType.MESH

N_X = 4
N_Y = 4
N_T = 4
N_REP = 8
BLOCK = 1024
FEAT = 256
TILE = 128
GRID = BLOCK // TILE
CAP = 32
SHARE = BLOCK // N_REP
PIECES = 2
PART_A = (48, 48)
PART_B = tuple(SHARE - rows for rows in PART_A)
GROWS = FEAT // 2 // N_REP


def rows_index(t, y, core):
    return (t * N_Y + y) * 2 + core


def layer_kernel(
    scale,
    fcount_ref,
    bcount_ref,
    fslots_hbm,
    bslots_hbm,
    order_hbm,
    feat_hbm,
    weight_hbm,
    cot_hbm,
    ftiles_hbm,
    btiles_hbm,
    lo_ref,
    gw_ref,
    gi_ref,
    slots_v,
    map_v,
    map_ref,
    order_v,
    feat_v,
    weight_v,
    cot_v,
    ftiles_v,
    btiles_v,
    dense,
    unperm,
    src,
    own,
    ya_f,
    ya_b,
    xa_f,
    xa_b,
    yb_f,
    yb_b,
    part,
    part_b,
    rsx_land,
    rsz_land,
    rs_mid,
    rsz_out,
    rs_land,
    share_v,
    gterm,
    gd_land,
    gmid,
    ga_land,
    gb_land,
    gc_land,
    ghalf,
    local_sem,
    ya_send,
    ya_recv,
    xa_send,
    xa_recv,
    za_send,
    za_recv,
    zb_send,
    zb_recv,
    yb_send,
    yb_recv,
    xb_send,
    xb_recv,
    side_send,
    side_recv,
    rsx_send,
    rsx_recv,
    rsz_send,
    rsz_recv,
    agz_send,
    rs_send,
    rs_recv,
    ag_send,
    ag_recv,
    ga_send,
    ga_recv,
    gb_send,
    gb_recv,
    gc_send,
    gc_recv,
    gd_send,
    gd_recv,
    ge_send,
    ge_recv,
    gf_send,
    gf_recv,
    out_sem,
):
    me = lax.axis_index("rows")
    rep = lax.axis_index("rep")
    core = lax.rem(me, 2)
    y = lax.rem(lax.div(me, 2), N_Y)
    t = lax.div(me, 2 * N_Y)
    x = lax.div(rep, 2)
    zl = lax.rem(rep, 2)
    other = 1 - core
    straight = core == zl
    crossed = jnp.logical_not(straight)
    blocks = [lax.rem(t + d, N_T) for d in (0, 1, 3, 2)]

    sibling = (rows_index(t, y, other), rep)

    def y_peer(d):
        return (rows_index(t, lax.rem(y + d, N_Y), core), rep)

    def cross_peer(d):
        return (rows_index(lax.rem(t + d, N_T), y, zl), x * 2 + core)

    def z_peer(d):
        return (rows_index(lax.rem(t + d, N_T), y, core), rep)

    def rep_index(d):
        dx, dz = d // 2, d % 2
        px = lax.rem(x + dx, N_X)
        pz = lax.rem(zl + dz, 2)
        return px * 2 + pz

    def rep_from(d):
        dx, dz = d // 2, d % 2
        return (lax.rem(x + N_X - dx, N_X)) * 2 + lax.rem(zl + dz, 2)

    def rep_peer(d):
        return (me, rep_index(d))

    def remote(source_ref, target_ref, send, recv, device):
        return pltpu.make_async_remote_copy(
            src_ref=source_ref,
            dst_ref=target_ref,
            send_sem=send,
            recv_sem=recv,
            device_id=device,
            device_id_type=MESH,
        )

    loads = [
        pltpu.make_async_copy(order_hbm, order_v, local_sem.at[0]),
        pltpu.make_async_copy(feat_hbm, feat_v, local_sem.at[1]),
        pltpu.make_async_copy(weight_hbm, weight_v, local_sem.at[2]),
        pltpu.make_async_copy(cot_hbm, cot_v, local_sem.at[3]),
        pltpu.make_async_copy(ftiles_hbm, ftiles_v.at[:, pl.ds(0, CAP)], local_sem.at[4]),
        pltpu.make_async_copy(btiles_hbm, btiles_v.at[:, pl.ds(0, CAP)], local_sem.at[5]),
        pltpu.make_async_copy(fslots_hbm, slots_v.at[0], local_sem.at[6]),
        pltpu.make_async_copy(bslots_hbm, slots_v.at[1], local_sem.at[7]),
    ]
    tiles = (ftiles_v, btiles_v)
    for held in tiles:
        for s in range(N_T):
            held[s, CAP] = jnp.zeros((TILE, TILE), BF16)
    for load in loads[:4] + loads[6:]:
        load.start()

    barrier = pltpu.get_barrier_semaphore()
    partners = [sibling]
    partners += [y_peer(d) for d in range(1, N_Y)]
    partners += [z_peer(d) for d in range(1, N_T)]
    partners += [cross_peer(d) for d in range(1, N_T)]
    partners += [rep_peer(d) for d in range(1, N_REP)]
    for partner in partners:
        pl.semaphore_signal(barrier, inc=1, device_id=partner, device_id_type=MESH)

    @pl.when(crossed)
    def _():
        pl.semaphore_signal(barrier, inc=1, device_id=cross_peer(0), device_id_type=MESH)

    def share_rows(index):
        return pl.ds(pl.multiple_of(index * SHARE, SHARE), SHARE)

    loads[0].wait()
    wanted = jnp.transpose(jnp.broadcast_to(order_v[0:1, share_rows(rep)], (SHARE, SHARE)))
    lanes = lax.broadcasted_iota(jnp.int32, (SHARE, TILE), 1)
    one_hot = jnp.concatenate(
        [jnp.where(wanted == lanes + b * TILE, 1.0, 0.0).astype(BF16) for b in range(GRID)], axis=1
    )
    loads[1].wait()
    own[0] = jnp.dot(one_hot, feat_v[...], preferred_element_type=F32).astype(BF16)
    ya_f[y] = own[0, 0 : PART_A[0], :]

    @pl.when(straight)
    def _():
        yb_f[y, t] = own[0, PART_A[0] : SHARE, :]
        pl.semaphore_wait(barrier, len(partners))

    @pl.when(crossed)
    def _():
        pl.semaphore_wait(barrier, len(partners) + 1)

    land_ya = (ya_f, ya_b)
    land_xa = (xa_f, xa_b)
    land_yb = (yb_f, yb_b)
    first_a = [pl.ds(0, rows) for rows in PART_A]
    last_b = [pl.ds(rows, SHARE - rows) for rows in PART_A]

    def ya_copy(p, d):
        ref = land_ya[p].at[y]
        return remote(ref, ref, ya_send.at[p, d], ya_recv.at[p, d], y_peer(d))

    def xa_copy(p, d):
        return remote(
            land_ya[p].at[lax.rem(x + d, N_X)], land_xa[p].at[x], xa_send.at[p, d], xa_recv.at[p, d], rep_peer(2 * d)
        )

    def za_copy(p, d):
        return remote(
            land_xa[p],
            src.at[p, t, :, zl, first_a[p], :],
            za_send.at[p, d],
            za_recv.at[p, d],
            cross_peer(d),
        )

    def zb_copy(p, d):
        return remote(
            own.at[p, last_b[p], :], land_yb[p].at[y, t], zb_send.at[p, d], zb_recv.at[p, d], cross_peer(d)
        )

    def yb_copy(p, i, d):
        ref = land_yb[p].at[y, blocks[i]]
        return remote(ref, ref, yb_send.at[p, i, d], yb_recv.at[p, i, d], y_peer(d))

    def xb_copy(p, i, d):
        return remote(
            land_yb[p].at[lax.rem(x + d, N_X), blocks[i]],
            src.at[p, blocks[i], x, core, last_b[p], :],
            xb_send.at[p, i, d],
            xb_recv.at[p, i, d],
            rep_peer(2 * d),
        )

    def side_copy(p, i):
        ref = src.at[p, blocks[i], :, core]
        return remote(ref, ref, side_send.at[p, i], side_recv.at[p, i], sibling)

    from_z = (0, 3, 1, 2)

    def begin(p):
        for d in (2, 1, 3):
            zb_copy(p, d).start()

        @pl.when(crossed)
        def _():
            zb_copy(p, 0).start()

        for d in (2, 1, 3):
            ya_copy(p, d).start()

    def z_wait(copy, i):
        if i == 0:

            @pl.when(crossed)
            def _():
                copy.wait_recv()

        else:
            copy.wait_recv()

    def a_over_x(p):
        for d in (1, 2, 3):
            ya_copy(p, d).wait_recv()
        for d in (2, 1, 3):
            xa_copy(p, d).start()
        land_xa[p][x] = land_ya[p][x]

    def a_over_z(p):
        for d in (1, 2, 3):
            xa_copy(p, d).wait_recv()
        for d in (2, 1, 3):
            za_copy(p, d).start()

        @pl.when(crossed)
        def _():
            za_copy(p, 0).start()

        @pl.when(straight)
        def _():
            src[p, t, :, zl, first_a[p], :] = land_xa[p][...]

    def b_over_y(p):
        for i in range(N_T):
            z_wait(zb_copy(p, from_z[i]), i)
            for d in (2, 1, 3):
                yb_copy(p, i, d).start()

    def b_over_x(p):
        for i in range(N_T):
            for d in (1, 2, 3):
                yb_copy(p, i, d).wait_recv()
            for d in (2, 1, 3):
                xb_copy(p, i, d).start()
            src[p, blocks[i], x, core, last_b[p], :] = land_yb[p][x, blocks[i]]

    def finish(p, i):
        for d in (1, 2, 3):
            xb_copy(p, i, d).wait_recv()
        z_wait(za_copy(p, from_z[i]), i)
        side_copy(p, i).start()

    def use_all(p):
        part[...] = jnp.zeros((BLOCK, FEAT), F32)

        @pl.loop(0, N_T)
        def _(i):
            block = lax.rem(t + i + i // 2 * (5 - 2 * i), N_T)
            ref = src.at[p, block, :, core]
            remote(ref, ref, side_send.at[p, i], side_recv.at[p, i], sibling).wait_recv()
            part[...] += jnp.dot(
                dense[p, block], src[p, block].reshape(BLOCK, FEAT), preferred_element_type=F32
            )

    def slot_maps():
        loads[6].wait()
        loads[7].wait()
        count_refs = (fcount_ref, bcount_ref)
        rows8 = lax.broadcasted_iota(jnp.int32, (2 * N_T, 1), 0)
        live = jnp.zeros((2 * N_T, 1), jnp.int32)
        for row in range(2 * N_T):
            live = jnp.where(rows8 == row, count_refs[row // N_T][row % N_T], live)
        keys = jnp.concatenate(
            [slots_v[p, s, 0:1, :] * GRID + slots_v[p, s, 1:2, :] for p in range(2) for s in range(N_T)],
            axis=0,
        )
        cells = lax.broadcasted_iota(jnp.int32, (2 * N_T, TILE), 1)
        found = jnp.full((2 * N_T, TILE), CAP, jnp.int32)
        for slot in range(CAP):
            hit = jnp.logical_and(keys[:, slot : slot + 1] == cells, live > slot)
            found = jnp.where(hit, slot, found)
        map_v[...] = found
        to_scalar = pltpu.make_async_copy(map_v, map_ref, local_sem.at[8])
        to_scalar.start()
        to_scalar.wait()

    def lay_out(p):
        loads[4 + p].wait()

        @pl.loop(0, N_T * GRID)
        def _(step):
            s = step // GRID
            a = step % GRID
            rows = pl.ds(pl.multiple_of(a * TILE, TILE), TILE)
            for b in range(GRID):
                slot = map_ref[p * N_T + s, a * GRID + b]
                dense[p, s, rows, pl.ds(b * TILE, TILE)] = tiles[p][s, slot]

    begin(0)
    loads[4].start()
    loads[5].start()
    loads[2].wait()
    loads[3].wait()
    own[1] = lax.dot_general(
        cot_v[share_rows(rep), :], weight_v[...], (((1,), (1,)), ((), ())), preferred_element_type=F32
    ).astype(BF16)
    ya_b[y] = own[1, 0 : PART_A[1], :]

    @pl.when(straight)
    def _():
        yb_b[y, t] = own[1, PART_A[1] : SHARE, :]

    begin(1)
    slot_maps()
    a_over_x(0)
    b_over_y(0)
    a_over_z(0)
    lay_out(0)
    b_over_x(0)
    lay_out(1)

    finish(0, 0)
    finish(0, 1)
    a_over_x(1)
    finish(0, 2)
    finish(0, 3)
    b_over_y(1)
    a_over_z(1)
    use_all(0)

    def pair_rows(index):
        return pl.ds(pl.multiple_of(index * 2 * SHARE, 2 * SHARE), 2 * SHARE)

    def rsx_copy(d):
        return remote(
            part_b.at[0, pair_rows(lax.rem(x + d, N_X)), :],
            rsx_land.at[d],
            rsx_send.at[d],
            rsx_recv.at[d],
            rep_peer(2 * d),
        )

    def rsz_copy():
        return remote(rsz_out, rsz_land, rsz_send.at[0], rsz_recv.at[0], rep_peer(1))

    part_b[0] = part[...].astype(BF16)
    for d in (2, 1, 3):
        rsx_copy(d).start()

    b_over_x(1)

    @pl.loop(0, GRID)
    def _(a):
        rows = pl.ds(pl.multiple_of(a * TILE, TILE), TILE)
        spots = lax.broadcasted_iota(jnp.int32, (TILE, BLOCK), 0) + a * TILE
        unperm[rows, :] = jnp.where(order_v[...] == spots, 1.0, 0.0).astype(BF16)

    total = part[pair_rows(x), :]
    for d in range(1, N_X):
        rsx_copy(d).wait_recv()
        total = total + rsx_land[d].astype(F32)
    rs_mid[...] = total
    rsz_out[...] = rs_mid[share_rows(1 - zl), :].astype(BF16)
    rsz_copy().start()

    finish(1, 0)
    finish(1, 1)

    partner = rep_index(1)

    def ag_own(d):
        return remote(
            share_v.at[0], lo_ref.at[share_rows(rep), :], ag_send.at[0, d], ag_recv.at[0, d], rep_peer(d)
        )

    def ag_pass(d):
        rows = share_rows(partner)
        return remote(
            lo_ref.at[rows, :], lo_ref.at[rows, :], agz_send.at[d], ag_recv.at[0, 2 * d + 1], rep_peer(2 * d)
        )

    rsz_copy().wait_recv()
    agg = (rs_mid[share_rows(zl), :] + rsz_land[...].astype(F32)).astype(BF16)
    share_v[0] = jnp.dot(agg, weight_v[...], preferred_element_type=F32).astype(BF16)
    for d in (1, 4, 2, 6):
        ag_own(d).start()
    lo_own = pltpu.make_async_copy(share_v.at[0], lo_ref.at[share_rows(rep), :], out_sem.at[0])
    lo_own.start()

    gterm[...] = lax.dot_general(
        agg, cot_v[share_rows(rep), :], (((0,), (0,)), ((), ())), preferred_element_type=F32
    )
    ghalf_rows = FEAT // 2

    def core_rows(index):
        return pl.ds(pl.multiple_of(index * ghalf_rows, ghalf_rows), ghalf_rows)

    def gd_copy():
        return remote(
            gterm.at[core_rows(other), :], gd_land, gd_send.at[0], gd_recv.at[0], sibling
        )

    def g_rows(index):
        return pl.ds(pl.multiple_of(index * GROWS, GROWS), GROWS)

    def ga_copy(d):
        return remote(
            gmid.at[g_rows(rep_index(d)), :],
            ga_land.at[d],
            ga_send.at[d],
            ga_recv.at[d],
            rep_peer(d),
        )

    def gb_copy(d):
        return remote(gb_land.at[y], gb_land.at[y], gb_send.at[d], gb_recv.at[d], y_peer(d))

    def gc_copy(d):
        return remote(gc_land.at[t], gc_land.at[t], gc_send.at[d], gc_recv.at[d], z_peer(d))

    def ge_copy(d):
        mine = ghalf.at[g_rows(rep), :]
        return remote(mine, mine, ge_send.at[d], ge_recv.at[d], rep_peer(d))

    def gf_copy():
        return remote(
            ghalf, gw_ref.at[core_rows(core), :], gf_send.at[0], gf_recv.at[0], sibling
        )

    gd_copy().start()

    finish(1, 2)
    finish(1, 3)
    gd_copy().wait_recv()
    gmid[...] = gterm[core_rows(core), :] + gd_land[...]
    for d in range(1, N_REP):
        ga_copy(d).start()

    use_all(1)
    part_b[1] = part[...].astype(BF16)
    part[...] = jnp.dot(unperm[...], part_b[1], preferred_element_type=F32)
    part_b[1] = part[...].astype(BF16)

    piece = SHARE // PIECES

    def piece_rows(index, h):
        return pl.ds(pl.multiple_of(index * SHARE + h * piece, piece), piece)

    def rs_copy(d, h):
        return remote(
            part_b.at[1, piece_rows(rep_index(d), h), :],
            rs_land.at[d, pl.ds(h * piece, piece)],
            rs_send.at[h, d],
            rs_recv.at[h, d],
            rep_peer(d),
        )

    def ag_copy(d, h):
        return remote(
            share_v.at[1, pl.ds(h * piece, piece)],
            gi_ref.at[piece_rows(rep, h), :],
            ag_send.at[1 + h, d],
            ag_recv.at[1 + h, d],
            rep_peer(d),
        )

    far_first = (5, 4, 3, 7, 2, 6, 1)
    for h in range(PIECES):
        for d in far_first:
            rs_copy(d, h).start()

    ag_own(1).wait_recv()
    for d in range(1, N_X):
        ag_pass(d).start()

    gsum = gmid[g_rows(rep), :]
    for d in range(1, N_REP):
        ga_copy(d).wait_recv()
        gsum = gsum + ga_land[d]
    gb_land[y] = gsum
    for d in range(1, N_Y):
        gb_copy(d).start()
    for d in range(1, N_Y):
        gb_copy(d).wait_recv()
    gc_land[t] = gb_land[0] + gb_land[1] + gb_land[2] + gb_land[3]
    for d in range(1, N_T):
        gc_copy(d).start()
    for d in range(1, N_T):
        gc_copy(d).wait_recv()
    ghalf[g_rows(rep), :] = (gc_land[0] + gc_land[1] + gc_land[2] + gc_land[3]) * scale
    for d in range(1, N_REP):
        ge_copy(d).start()

    for h in range(PIECES):
        back_total = part[piece_rows(rep, h), :]
        for d in range(1, N_REP):
            rs_copy(d, h).wait_recv()
            back_total = back_total + rs_land[d, h * piece : (h + 1) * piece].astype(F32)
        keep = feat_v[piece_rows(rep, h), :].astype(F32) > 0.0
        share_v[1, h * piece : (h + 1) * piece] = jnp.where(keep, back_total, 0.0).astype(BF16)
        for d in far_first:
            ag_copy(d, h).start()
    gi_own = pltpu.make_async_copy(share_v.at[1], gi_ref.at[share_rows(rep), :], out_sem.at[1])
    gi_own.start()

    for d in range(1, N_REP):
        ge_copy(d).wait_recv()
    gf_copy().start()
    gw_own = pltpu.make_async_copy(ghalf, gw_ref.at[core_rows(core), :], out_sem.at[2])
    gw_own.start()

    for p in range(2):

        @pl.when(crossed)
        def _():
            zb_copy(p, 0).wait_send()
            za_copy(p, 0).wait_send()

        for d in (1, 2, 3):
            ya_copy(p, d).wait_send()
            xa_copy(p, d).wait_send()
            za_copy(p, d).wait_send()
            zb_copy(p, d).wait_send()
            for i in range(N_T):
                yb_copy(p, i, d).wait_send()
                xb_copy(p, i, d).wait_send()
        for i in range(N_T):
            side_copy(p, i).wait_send()
    for d in (1, 2, 4, 6):
        ag_own(d).wait_send()
    for d in range(1, N_X):
        rsx_copy(d).wait_send()
        ag_pass(d).wait_send()
    rsz_copy().wait_send()
    for d in range(1, N_REP):
        for h in range(PIECES):
            rs_copy(d, h).wait_send()
        ga_copy(d).wait_send()
    for d in range(1, N_Y):
        gb_copy(d).wait_send()
    for d in range(1, N_T):
        gc_copy(d).wait_send()
    gd_copy().wait_send()

    for d in (2, 4, 6, 3, 5, 7):
        ag_own(d).wait_recv()
    for d in range(1, N_REP):
        for h in range(PIECES):
            ag_copy(d, h).wait_recv()
    gf_copy().wait_recv()
    lo_own.wait()
    gi_own.wait()
    gw_own.wait()
    for d in range(1, N_REP):
        for h in range(PIECES):
            ag_copy(d, h).wait_send()
        ge_copy(d).wait_send()
    gf_copy().wait_send()

def copy_kernel(*refs):
    sources, targets, held, sems = refs[:3], refs[3:6], refs[6:9], refs[9]
    pieces = []
    for n in range(3):
        rows = sources[n].shape[0] // 4
        for c in range(4):
            part = pl.ds(c * rows, rows)
            sem = sems.at[n * 4 + c]
            inward = pltpu.make_async_copy(sources[n].at[part], held[n].at[part], sem)
            inward.start()
            pieces.append((inward, pltpu.make_async_copy(held[n].at[part], targets[n].at[part], sem)))
    for inward, outward in pieces:
        inward.wait()
        outward.start()
    for _, outward in pieces:
        outward.wait()


def body(
    features,
    weight,
    cotangent,
    node_order,
    forward_tiles,
    forward_slots,
    forward_count,
    backward_tiles,
    backward_slots,
    backward_count,
):
    scale = 1.0 / math.sqrt(BLOCK * lax.axis_size("rows"))
    any_spec = pl.BlockSpec(memory_space=pl.ANY)
    dma = pltpu.SemaphoreType.DMA

    def kernel(*refs):
        layer_kernel(scale, *refs)

    results = pl.pallas_call(
        kernel,
        out_shape=[
            jax.ShapeDtypeStruct((BLOCK, FEAT), BF16),
            jax.ShapeDtypeStruct((FEAT, FEAT), F32),
            jax.ShapeDtypeStruct((BLOCK, FEAT), BF16),
        ],
        in_specs=[pl.BlockSpec(memory_space=pltpu.SMEM)] * 2 + [any_spec] * 8,
        out_specs=[any_spec] * 3,
        scratch_shapes=[
            pltpu.VMEM((2, N_T, 2, CAP), jnp.int32),
            pltpu.VMEM((2 * N_T, TILE), jnp.int32),
            pltpu.SMEM((2 * N_T, TILE), jnp.int32),
            pltpu.VMEM((1, BLOCK), jnp.int32),
            pltpu.VMEM((BLOCK, FEAT), BF16),
            pltpu.VMEM((FEAT, FEAT), BF16),
            pltpu.VMEM((BLOCK, FEAT), BF16),
            pltpu.VMEM((N_T, CAP + 1, TILE, TILE), BF16),
            pltpu.VMEM((N_T, CAP + 1, TILE, TILE), BF16),
            pltpu.VMEM((2, N_T, BLOCK, BLOCK), BF16),
            pltpu.VMEM((BLOCK, BLOCK), BF16),
            pltpu.VMEM((2, N_T, N_X, 2, SHARE, FEAT), BF16),
            pltpu.VMEM((2, SHARE, FEAT), BF16),
            pltpu.VMEM((N_Y, PART_A[0], FEAT), BF16),
            pltpu.VMEM((N_Y, PART_A[1], FEAT), BF16),
            pltpu.VMEM((N_X, PART_A[0], FEAT), BF16),
            pltpu.VMEM((N_X, PART_A[1], FEAT), BF16),
            pltpu.VMEM((N_Y, N_T, PART_B[0], FEAT), BF16),
            pltpu.VMEM((N_Y, N_T, PART_B[1], FEAT), BF16),
            pltpu.VMEM((BLOCK, FEAT), F32),
            pltpu.VMEM((2, BLOCK, FEAT), BF16),
            pltpu.VMEM((N_X, 2 * SHARE, FEAT), BF16),
            pltpu.VMEM((SHARE, FEAT), BF16),
            pltpu.VMEM((2 * SHARE, FEAT), F32),
            pltpu.VMEM((SHARE, FEAT), BF16),
            pltpu.VMEM((N_REP, SHARE, FEAT), BF16),
            pltpu.VMEM((2, SHARE, FEAT), BF16),
            pltpu.VMEM((FEAT, FEAT), F32),
            pltpu.VMEM((FEAT // 2, FEAT), F32),
            pltpu.VMEM((FEAT // 2, FEAT), F32),
            pltpu.VMEM((N_REP, GROWS, FEAT), F32),
            pltpu.VMEM((N_Y, GROWS, FEAT), F32),
            pltpu.VMEM((N_T, GROWS, FEAT), F32),
            pltpu.VMEM((FEAT // 2, FEAT), F32),
            dma((9,)),
            dma((2, N_Y)),
            dma((2, N_Y)),
            dma((2, N_Y)),
            dma((2, N_Y)),
            dma((2, N_Y)),
            dma((2, N_Y)),
            dma((2, N_Y)),
            dma((2, N_Y)),
            dma((2, N_T, N_Y)),
            dma((2, N_T, N_Y)),
            dma((2, N_T, N_Y)),
            dma((2, N_T, N_Y)),
            dma((2, N_T)),
            dma((2, N_T)),
            dma((N_X,)),
            dma((N_X,)),
            dma((1,)),
            dma((1,)),
            dma((N_X,)),
            dma((PIECES, N_REP)),
            dma((PIECES, N_REP)),
            dma((1 + PIECES, N_REP)),
            dma((1 + PIECES, N_REP)),
            dma((N_REP,)),
            dma((N_REP,)),
            dma((N_Y,)),
            dma((N_Y,)),
            dma((N_T,)),
            dma((N_T,)),
            dma((1,)),
            dma((1,)),
            dma((N_REP,)),
            dma((N_REP,)),
            dma((1,)),
            dma((1,)),
            dma((3,)),
        ],
        compiler_params=pltpu.CompilerParams(
            collective_id=0, has_side_effects=True, vmem_limit_bytes=56 * 1024 * 1024
        ),
    )(
        forward_count[0, 0],
        backward_count[0, 0],
        forward_slots[0, 0],
        backward_slots[0, 0],
        node_order,
        features,
        weight,
        cotangent,
        forward_tiles[0, 0],
        backward_tiles[0, 0],
    )
    return pl.pallas_call(
        copy_kernel,
        out_shape=[jax.ShapeDtypeStruct(r.shape, r.dtype) for r in results],
        in_specs=[any_spec] * 3,
        out_specs=[any_spec] * 3,
        scratch_shapes=[pltpu.VMEM(r.shape, r.dtype) for r in results] + [dma((12,))],
        compiler_params=pltpu.CompilerParams(vmem_limit_bytes=56 * 1024 * 1024),
    )(*results)


def solution(mesh):
    placed = (
        P("rows", None),
        P(),
        P("rows", None),
        P("rows", None),
        P("rows", "rep", None, None, None, None),
        P("rows", "rep", None, None, None),
        P("rows", "rep", None),
        P("rows", "rep", None, None, None, None),
        P("rows", "rep", None, None, None),
        P("rows", "rep", None),
    )
    return jax.shard_map(
        body,
        mesh=mesh,
        in_specs=placed,
        out_specs=(P("rows", None), P(), P("rows", None)),
        check_vma=False,
    )
```
